32 devices in a mesh: ctx: 4 (over y, x), tp: 8 (over z, core).
Axes of the slice: x: 2, y: 2, z: 4, core: 2. Of those that a mesh axis runs over, the one named last changes fastest.
Arguments:
- short_query: bfloat16 [4096, 8192], P('tp', 'ctx'), may hold values from -16 to 16
- short_key: bfloat16 [4096, 8192], P('tp', 'ctx'), may hold values from -6 to 6
- short_value: bfloat16 [4096, 8192], P('tp', 'ctx'), may hold values from -6 to 6
- short_taps: bfloat16 [4096, 128], P('tp'), may hold values from -0.5 to 0.5
- norm_gain: float32 [4096], P('tp'), may hold values from 0.1 to 1.9
- long_key: bfloat16 [4096, 8192], P('tp', 'ctx'), may hold values from -6 to 6
- long_query: bfloat16 [4096, 8192], P('tp', 'ctx'), may hold values from -6 to 6
- residues: float32 [16, 4096], P(None, 'tp'), may hold values from -1.5 to 1.5
- decay_rates: float32 [16, 4096], P(None, 'tp'), may hold values from 6.1035156e-05 to 0.05
Outputs:
- mixer_output: float32 [4096, 8192], P('tp', 'ctx')
The draws below stay inside these ranges and needn't reach their ends.
All inputs are finite; a program needn't handle non-finite values.
Results may differ from the reference program's by a relative error of at most 0.0029.
Values may be sent and summed in bfloat16 or wider, within the bound.
A program may use at most 128 MiB of HBM per device.

```python
import math
import jax
import jax.numpy as jnp
from jax import lax

D = 4096
TAPS = 128
MODES = 16
SEQ = 8192


def draw_short_query(key, part):
    value_key = jax.random.fold_in(key, 0)
    channel = jnp.arange(D).astype(jnp.float32)[:, None]
    rising = jnp.sqrt(1.0 + 2.0 * channel / D)
    values = jnp.clip(jax.random.normal(value_key, (D, SEQ), jnp.float32), -4.0, 4.0)
    return (values * rising).astype(jnp.bfloat16)


def block_levels(rng, shape, shards, low, top_value):
    level = 1.0
    for axis_at, blocks in shards:
        steps = jax.random.uniform(jax.random.fold_in(jax.random.fold_in(rng, 6), axis_at), (blocks,), jnp.float32, low / len(shards), top_value / len(shards))
        level = level * jnp.repeat(jnp.exp(steps), shape[axis_at] // blocks).reshape((-1,) + (1,) * (len(shape) - 1 - axis_at))
    return level


def bell_draw(stream_key, extent, deviation, most, shards=(), held_as=jnp.bfloat16):
    gain = block_levels(stream_key, extent, shards, -0.22, 0.18) if shards else 1.0
    entries = jax.random.normal(stream_key, extent, jnp.float32) * deviation * gain
    return jnp.minimum(jnp.maximum(entries, -most), most).astype(held_as)


def setup_inputs(seed: int = 0) -> dict:
    seeds = jax.random.split(jax.random.key(seed), 10)
    return {
        "short_query": draw_short_query(jax.random.fold_in(seeds[9], 71), 0),
        "short_key": bell_draw(seeds[1], (D, SEQ), 1.0, 6.0, ((0, 8), (1, 4))),
        "short_value": bell_draw(seeds[2], (D, SEQ), 1.0, 6.0, ((0, 8), (1, 4))),
        "short_taps": bell_draw(seeds[3], (D, TAPS), TAPS ** -0.5, 0.5, ((0, 8),)),
        "norm_gain": jnp.clip(1.0 + 0.18 * jax.random.normal(seeds[4], (D,), jnp.float32), 0.1, 1.9),
        "long_key": bell_draw(seeds[5], (D, SEQ), 1.0, 6.0, ((0, 8), (1, 4))),
        "long_query": bell_draw(seeds[6], (D, SEQ), 1.0, 6.0, ((0, 8), (1, 4))),
        "residues": bell_draw(seeds[7], (MODES, D), MODES ** -0.5, 1.5, ((1, 8),), jnp.float32),
        "decay_rates": jnp.clip(jnp.exp(math.log(0.05) - 6.7083283 * jax.random.uniform(seeds[8], (MODES, D), jnp.float32) ** block_levels(seeds[8], (MODES, D), ((1, 8),), -0.2, 0.2)), 6.103515625e-05, 0.05),
    }


def make_band(filter_taps):
    tap_count = filter_taps.shape[1]
    row_index = jnp.arange(tap_count)[:, None]
    col_index = jnp.arange(2 * tap_count)[None, :]
    lag_index = row_index + tap_count - col_index
    inside = (lag_index >= 0) & (lag_index < tap_count)
    picked = jnp.take(filter_taps, jnp.clip(lag_index, 0, tap_count - 1), axis=1)
    return jnp.where(inside[None, :, :], picked, jnp.zeros_like(picked))

def short_block(operands):
    extended, filter_taps = operands
    tap_count = filter_taps.shape[1]
    channels, span_len = extended.shape
    length = span_len - tap_count
    block_count = length // tap_count
    earlier = extended[:, :length].reshape(channels, block_count, tap_count)
    current = extended[:, tap_count:].reshape(channels, block_count, tap_count)
    windows = jnp.concatenate([earlier, current], axis=2).astype(jnp.float32)
    band_rows = make_band(filter_taps).astype(jnp.float32)
    mixed = jnp.einsum('cbm,cim->cbi', windows, band_rows, precision=lax.Precision.HIGHEST)
    return mixed.reshape(channels, length)

def long_block(operands):
    signal, residue, decays = operands
    length = signal.shape[1]
    offsets = jnp.arange(length).astype(jnp.float32)
    weights = residue * jnp.sqrt(-jnp.expm1(-2.0 * decays))
    kernel = lax.optimization_barrier(jnp.sum(weights[:, :, None] * jnp.exp(-decays[:, :, None] * offsets[None, None, :]), axis=0))
    spectrum = jnp.fft.rfft(signal, n=2 * length, axis=1) * jnp.fft.rfft(kernel, n=2 * length, axis=1)
    return jnp.fft.irfft(spectrum, n=2 * length, axis=1)[:, :length]

def reference(short_query, short_key, short_value, short_taps, norm_gain, long_key, long_query, residues, decay_rates):
    channels, length = short_value.shape
    tap_count = short_taps.shape[1]
    first_product = (short_key.astype(jnp.float32) * short_value.astype(jnp.float32)).astype(jnp.bfloat16)
    first_product = lax.optimization_barrier(first_product)
    extended = jnp.concatenate([jnp.zeros((channels, tap_count), jnp.bfloat16), first_product], axis=1)
    group_size = min(256, channels)
    group_count = channels // group_size
    short_mix = lax.map(short_block, (extended.reshape(group_count, group_size, length + tap_count), short_taps.reshape(group_count, group_size, tap_count)))
    short_mix = short_mix.reshape(channels, length)
    gated = short_query.astype(jnp.float32) * short_mix
    mean_square = lax.optimization_barrier(jnp.mean(gated * gated, axis=0))
    normed = gated * norm_gain[:, None] * lax.rsqrt(mean_square + 1e-06)[None, :]
    long_input = long_key.astype(jnp.float32) * normed
    mode_count = residues.shape[0]
    lane_count = min(64, channels)
    lane_groups = channels // lane_count
    residue_blocks = residues.reshape(mode_count, lane_groups, lane_count).transpose(1, 0, 2)
    decay_blocks = decay_rates.reshape(mode_count, lane_groups, lane_count).transpose(1, 0, 2)
    long_mix = lax.map(long_block, (long_input.reshape(lane_groups, lane_count, length), residue_blocks, decay_blocks))
    long_mix = long_mix.reshape(channels, length)
    return long_query.astype(jnp.float32) * long_mix
```

```python
import functools

import jax
import jax.numpy as jnp
from jax import lax
from jax.experimental import pallas as pl
from jax.experimental.pallas import tpu as pltpu
from jax.sharding import PartitionSpec as P

F32 = jnp.float32
BF16 = jnp.bfloat16
SUB = 8


def fused(
    n_ctx,
    n_tp,
    width,
    sq_hbm,
    sk_hbm,
    sv_hbm,
    lk_hbm,
    lq_hbm,
    taps_ref,
    gain_ref,
    decay_ref,
    weight_ref,
    out_hbm,
    sq,
    sk,
    sv,
    lk,
    lq,
    key_edge,
    value_edge,
    edge_send,
    edge_recv,
    gated,
    squares,
    sums,
    signal,
    tails,
    heads,
    bands,
    carry,
    states,
    in_sem,
    edge_in_sem,
    out_sem,
    edge_sem,
    sum_send_sem,
    sum_recv_sem,
    state_send_sem,
    state_recv_sem,
):
    channels, length = gated.shape
    block = taps_ref.shape[1]
    blocks = length // block
    groups = channels // SUB
    chunks = in_sem.shape[1]
    chunk_rows = channels // chunks
    pairs = chunk_rows // 16
    my_ctx = lax.axis_index("ctx")
    my_tp = lax.axis_index("tp")

    def edge_in(which, source, target):
        return pltpu.make_async_copy(
            source.at[:, pl.ds(length - block, block)], target, edge_in_sem.at[which]
        )

    def bring(which, source, target, chunk):
        rows = pl.ds(pl.multiple_of(chunk * chunk_rows, 16), chunk_rows)
        return pltpu.make_async_copy(source.at[rows], target.at[rows], in_sem.at[which, chunk])

    edge_in(0, sk_hbm, key_edge).start()
    edge_in(1, sv_hbm, value_edge).start()

    def start_short(chunk, _):
        bring(0, sk_hbm, sk, chunk).start()
        bring(1, sv_hbm, sv, chunk).start()
        bring(2, sq_hbm, sq, chunk).start()
        return 0

    def start_long(chunk, _):
        bring(3, lk_hbm, lk, chunk).start()
        bring(4, lq_hbm, lq, chunk).start()
        return 0

    lax.fori_loop(0, chunks, start_short, 0)
    lax.fori_loop(0, chunks, start_long, 0)

    barrier = pltpu.get_barrier_semaphore()

    def greet_ctx(step, _):
        other = lax.rem(my_ctx + step, n_ctx)
        pl.semaphore_signal(
            barrier, inc=1, device_id={"ctx": other}, device_id_type=pl.DeviceIdType.MESH
        )
        return 0

    def greet_tp(step, _):
        other = lax.rem(my_tp + step, n_tp)
        pl.semaphore_signal(
            barrier, inc=1, device_id={"tp": other}, device_id_type=pl.DeviceIdType.MESH
        )
        return 0

    lax.fori_loop(1, n_ctx, greet_ctx, 0)
    lax.fori_loop(1, n_tp, greet_tp, 0)
    pl.semaphore_wait(barrier, n_ctx + n_tp - 2)

    edge_in(0, sk_hbm, key_edge).wait()
    edge_in(1, sv_hbm, value_edge).wait()
    edge_send[...] = (key_edge[...].astype(F32) * value_edge[...].astype(F32)).astype(BF16)
    edge_copy = pltpu.make_async_remote_copy(
        src_ref=edge_send,
        dst_ref=edge_recv,
        send_sem=edge_sem.at[0],
        recv_sem=edge_sem.at[1],
        device_id={"ctx": lax.rem(my_ctx + 1, n_ctx)},
        device_id_type=pl.DeviceIdType.MESH,
    )
    edge_copy.start()

    row_id = lax.broadcasted_iota(jnp.int32, (block, block), 0)
    col_id = lax.broadcasted_iota(jnp.int32, (block, block), 1)
    lower_mask = jnp.where(col_id >= row_id, 1.0, 0.0).astype(BF16)
    upper_mask = jnp.where(col_id < row_id, 1.0, 0.0).astype(BF16)
    pick_row = lax.broadcasted_iota(jnp.int32, (16, block), 0) % SUB
    row_masks = [jnp.where(pick_row == c, 1.0, 0.0).astype(BF16) for c in range(SUB)]
    sub_id = lax.broadcasted_iota(jnp.int32, (SUB, block), 0)
    lane_id = lax.broadcasted_iota(jnp.int32, (SUB, block), 1)
    own_modes = (lane_id // (block // SUB)) == sub_id

    def spread(stacked):
        rows = stacked.shape[0]
        tiled = stacked.reshape(rows // 16, 16, block)
        return jnp.concatenate(
            [(tiled * row_masks[c][None]).reshape(rows, block) for c in range(SUB)], axis=1
        )

    def circulant(row):
        whole = jnp.broadcast_to(row, (block, block))
        return pltpu.roll(whole, 0, 1, stride=1, stride_axis=0).astype(BF16)

    def parts(value):
        high = value.astype(BF16)
        return high, (value - high.astype(F32)).astype(BF16)

    def at(b):
        return slice(b * block, (b + 1) * block)

    def over(b):
        return slice(b * SUB, (b + 1) * SUB)

    squares[...] = jnp.zeros_like(squares)
    edge_copy.wait()
    has_left = jnp.where(my_ctx > 0, 1.0, 0.0).astype(F32)

    def short_pair(pair, _):
        rows = pl.ds(pl.multiple_of(pair * 16, 16), 16)
        product = sk[rows, :].astype(F32) * sv[rows, :].astype(F32)
        query = sq[rows, :].astype(F32)
        edge = edge_recv[rows, :].astype(F32) * has_left
        taps = taps_ref[rows, :].astype(F32)
        for half in range(2):
            own = slice(half * SUB, (half + 1) * SUB)
            stacked = jnp.concatenate(
                [edge[own]]
                + [product[own, at(b)] for b in range(blocks)]
                + [jnp.zeros((SUB, block), F32)],
                axis=0,
            ).astype(BF16)
            bands_now = []
            for c in range(SUB):
                turned = circulant(taps[half * SUB + c : half * SUB + c + 1])
                bands_now.append(
                    jnp.concatenate([turned * lower_mask, turned * upper_mask], axis=1)
                )
            mixed = jnp.dot(
                spread(stacked),
                jnp.concatenate(bands_now, axis=0),
                preferred_element_type=F32,
            )
            place = pl.ds(pl.multiple_of(pair * 16 + half * SUB, SUB), SUB)
            for b in range(blocks):
                mix = mixed[over(b + 1), :block] + mixed[over(b), block:]
                gate = query[own, at(b)] * mix
                gated[place, at(b)] = gate
                squares[:, at(b)] += gate * gate
        return 0

    def short_chunk(chunk, _):
        bring(0, sk_hbm, sk, chunk).wait()
        bring(1, sv_hbm, sv, chunk).wait()
        bring(2, sq_hbm, sq, chunk).wait()
        lax.fori_loop(chunk * pairs, (chunk + 1) * pairs, short_pair, 0)
        return 0

    lax.fori_loop(0, chunks, short_chunk, 0)

    sums[my_tp] = jnp.sum(squares[...], axis=0, keepdims=True)

    def sum_copy(slot, other):
        return pltpu.make_async_remote_copy(
            src_ref=sums.at[slot],
            dst_ref=sums.at[slot],
            send_sem=sum_send_sem.at[other],
            recv_sem=sum_recv_sem.at[slot],
            device_id={"tp": other},
            device_id_type=pl.DeviceIdType.MESH,
        )

    def sum_start(step, _):
        sum_copy(my_tp, lax.rem(my_tp + step, n_tp)).start()
        return 0

    lax.fori_loop(1, n_tp, sum_start, 0)

    step_at = col_id.astype(F32)

    def make_params(g, _):
        decay = jnp.broadcast_to(decay_ref[pl.ds(g, 1), :], (block, block)).T
        weight = jnp.broadcast_to(weight_ref[pl.ds(g, 1), :], (block, block)).T
        tails[g] = jnp.concatenate(parts(jnp.exp(-decay * (block - 1 - step_at))), axis=1)
        kernel = weight * jnp.exp(-decay * step_at)
        high, low = parts(weight * jnp.exp(-decay * (step_at + 1.0)))
        heads[g] = jnp.concatenate([high, high, low], axis=0)
        modes = block // SUB
        for c in range(SUB):
            row = jnp.sum(kernel[c * modes : (c + 1) * modes], axis=0, keepdims=True)
            bands[g, c * block : (c + 1) * block, :] = circulant(row) * lower_mask
        return 0

    lax.fori_loop(0, groups, make_params, 0)

    def sum_wait(step, _):
        other = lax.rem(my_tp + step, n_tp)
        sum_copy(my_tp, other).wait_send()
        sum_copy(other, other).wait_recv()
        return 0

    lax.fori_loop(1, n_tp, sum_wait, 0)
    total = sums[0]
    for other in range(1, n_tp):
        total = total + sums[other]
    squares[...] = jnp.broadcast_to(lax.rsqrt(total / width + 1e-06), squares.shape)

    def state_pair(pair, _):
        rows = pl.ds(pl.multiple_of(pair * 16, 16), 16)
        key = lk[rows, :].astype(F32)
        for half in range(2):
            own = slice(half * SUB, (half + 1) * SUB)
            g = pair * 2 + half
            place = pl.ds(pl.multiple_of(pair * 16 + half * SUB, SUB), SUB)
            gain = gain_ref[place, :]
            stacked = jnp.concatenate(
                [
                    key[own, at(b)] * (gated[place, at(b)] * gain * squares[:, at(b)])
                    for b in range(blocks)
                ],
                axis=0,
            ).astype(BF16)
            signal[g] = stacked
            ends = lax.dot_general(
                jnp.concatenate([stacked, stacked], axis=1),
                tails[g],
                (((1,), (1,)), ((), ())),
                preferred_element_type=F32,
            )
            fade = jnp.exp(-decay_ref[pl.ds(g, 1), :] * block)
            state = jnp.zeros((SUB, block), F32)
            for b in range(blocks):
                carry[g, over(b), :] = state
                state = fade * state + jnp.where(own_modes, ends[over(b)], 0.0)
            states[my_ctx, pl.ds(g, 1), :] = jnp.sum(state, axis=0, keepdims=True)
        return 0

    def state_chunk(chunk, _):
        bring(3, lk_hbm, lk, chunk).wait()
        lax.fori_loop(chunk * pairs, (chunk + 1) * pairs, state_pair, 0)
        return 0

    lax.fori_loop(0, chunks, state_chunk, 0)

    def state_copy(slot, other):
        return pltpu.make_async_remote_copy(
            src_ref=states.at[slot],
            dst_ref=states.at[slot],
            send_sem=state_send_sem.at[other],
            recv_sem=state_recv_sem.at[slot],
            device_id={"ctx": other},
            device_id_type=pl.DeviceIdType.MESH,
        )

    def state_start(step, _):
        state_copy(my_ctx, lax.rem(my_ctx + step, n_ctx)).start()
        return 0

    lax.fori_loop(1, n_ctx, state_start, 0)

    def inner_group(g, _):
        place = pl.ds(pl.multiple_of(g * SUB, SUB), SUB)
        inner = jnp.dot(spread(signal[g]), bands[g], preferred_element_type=F32)
        for b in range(blocks):
            gated[place, at(b)] = inner[over(b)]
        return 0

    lax.fori_loop(0, groups, inner_group, 0)

    def state_wait(step, _):
        other = lax.rem(my_ctx + step, n_ctx)
        state_copy(my_ctx, other).wait_send()
        state_copy(other, other).wait_recv()
        return 0

    lax.fori_loop(1, n_ctx, state_wait, 0)

    entering = jnp.zeros(decay_ref.shape, F32)
    device_fade = jnp.exp(-decay_ref[...] * length)
    for other in range(n_ctx - 1):
        further = device_fade * entering + states[other]
        entering = jnp.where(other < my_ctx, further, entering)
    states[0] = entering

    def out_copy(chunk):
        rows = pl.ds(pl.multiple_of(chunk * chunk_rows, 16), chunk_rows)
        return pltpu.make_async_copy(gated.at[rows], out_hbm.at[rows], out_sem.at[chunk])

    def last_pair(pair, _):
        rows = pl.ds(pl.multiple_of(pair * 16, 16), 16)
        query = lq[rows, :].astype(F32)
        for half in range(2):
            own = slice(half * SUB, (half + 1) * SUB)
            g = pair * 2 + half
            place = pl.ds(pl.multiple_of(pair * 16 + half * SUB, SUB), SUB)
            fade = jnp.exp(-decay_ref[pl.ds(g, 1), :] * block)
            here = jnp.where(own_modes, states[0, pl.ds(g, 1), :], 0.0)
            before = []
            for b in range(blocks):
                before.append(carry[g, over(b), :] + here)
                here = here * fade
            high, low = parts(jnp.concatenate(before, axis=0))
            carried = jnp.dot(
                jnp.concatenate([high, low, high], axis=1),
                heads[g],
                preferred_element_type=F32,
            )
            for b in range(blocks):
                gated[place, at(b)] = query[own, at(b)] * (gated[place, at(b)] + carried[over(b)])
        return 0

    def last_chunk(chunk, _):
        bring(4, lq_hbm, lq, chunk).wait()
        lax.fori_loop(chunk * pairs, (chunk + 1) * pairs, last_pair, 0)
        out_copy(chunk).start()
        return 0

    lax.fori_loop(0, chunks, last_chunk, 0)

    def out_wait(chunk, _):
        out_copy(chunk).wait()
        return 0

    lax.fori_loop(0, chunks, out_wait, 0)


def shards(
    short_query,
    short_key,
    short_value,
    short_taps,
    norm_gain,
    long_key,
    long_query,
    residues,
    decay_rates,
):
    channels, length = short_value.shape
    block = short_taps.shape[1]
    modes = decay_rates.shape[0]
    groups = channels // SUB
    assert modes * SUB == block
    n_ctx, n_tp = lax.axis_size("ctx"), lax.axis_size("tp")
    chunks = min(8, channels // 16)
    weights = residues * jnp.sqrt(-jnp.expm1(-2.0 * decay_rates))
    decays = decay_rates.T.reshape(groups, block)
    weights = weights.T.reshape(groups, block)
    gains = jnp.broadcast_to(norm_gain[:, None], (channels, block))
    hbm = pl.BlockSpec(memory_space=pl.ANY)
    vmem = pl.BlockSpec(memory_space=pltpu.VMEM)
    dma = pltpu.SemaphoreType.DMA
    return pl.pallas_call(
        functools.partial(fused, n_ctx, n_tp, channels * n_tp),
        out_shape=jax.ShapeDtypeStruct((channels, length), F32),
        in_specs=[hbm] * 5 + [vmem] * 4,
        out_specs=hbm,
        scratch_shapes=[pltpu.VMEM((channels, length), BF16)] * 5
        + [pltpu.VMEM((channels, block), BF16)] * 4
        + [
            pltpu.VMEM((channels, length), F32),
            pltpu.VMEM((SUB, length), F32),
            pltpu.VMEM((n_tp, 1, length), F32),
            pltpu.VMEM((groups, block, block), BF16),
            pltpu.VMEM((groups, block, 2 * block), BF16),
            pltpu.VMEM((groups, 3 * block, block), BF16),
            pltpu.VMEM((groups, SUB * block, block), BF16),
            pltpu.VMEM((groups, block, block), F32),
            pltpu.VMEM((n_ctx, groups, block), F32),
            dma((5, chunks)),
            dma((2,)),
            dma((chunks,)),
            dma((2,)),
            dma((n_tp,)),
            dma((n_tp,)),
            dma((n_ctx,)),
            dma((n_ctx,)),
        ],
        compiler_params=pltpu.CompilerParams(
            collective_id=0, has_side_effects=True, vmem_limit_bytes=56 * 1024 * 1024
        ),
    )(
        short_query,
        short_key,
        short_value,
        long_key,
        long_query,
        short_taps,
        gains,
        decays,
        weights,
    )


def solution(mesh):
    in_specs = (
        P("tp", "ctx"),
        P("tp", "ctx"),
        P("tp", "ctx"),
        P("tp", None),
        P("tp"),
        P("tp", "ctx"),
        P("tp", "ctx"),
        P(None, "tp"),
        P(None, "tp"),
    )
    out_specs = P("tp", "ctx")
    return jax.shard_map(shards, mesh=mesh, in_specs=in_specs, out_specs=out_specs, check_vma=False)
```

```python
import functools

import jax
import jax.numpy as jnp
from jax import lax
from jax.experimental import pallas as pl
from jax.experimental.pallas import tpu as pltpu
from jax.sharding import PartitionSpec as P

F32 = jnp.float32
BF16 = jnp.bfloat16
SUB = 8


def fused(
    n_ctx,
    n_tp,
    width,
    sq_hbm,
    sk_hbm,
    sv_hbm,
    lk_hbm,
    lq_hbm,
    taps_ref,
    gain_ref,
    decay_ref,
    weight_ref,
    out_hbm,
    sq,
    sk,
    sv,
    lk,
    lq,
    key_edge,
    value_edge,
    edge_send,
    edge_recv,
    gated,
    squares,
    sums,
    signal,
    tails,
    heads,
    bands,
    carry,
    states,
    in_sem,
    edge_in_sem,
    out_sem,
    edge_sem,
    sum_send_sem,
    sum_recv_sem,
    state_send_sem,
    state_recv_sem,
):
    channels, length = gated.shape
    block = taps_ref.shape[1]
    blocks = length // block
    groups = channels // SUB
    chunks = in_sem.shape[1]
    chunk_rows = channels // chunks
    pairs = chunk_rows // 16
    my_ctx = lax.axis_index("ctx")
    my_tp = lax.axis_index("tp")

    def edge_in(which, source, target):
        return pltpu.make_async_copy(
            source.at[:, pl.ds(length - block, block)], target, edge_in_sem.at[which]
        )

    def bring(which, source, target, chunk):
        rows = pl.ds(pl.multiple_of(chunk * chunk_rows, 16), chunk_rows)
        return pltpu.make_async_copy(source.at[rows], target.at[rows], in_sem.at[which, chunk])

    edge_in(0, sk_hbm, key_edge).start()
    edge_in(1, sv_hbm, value_edge).start()

    def start_short(chunk, _):
        bring(0, sk_hbm, sk, chunk).start()
        bring(1, sv_hbm, sv, chunk).start()
        bring(2, sq_hbm, sq, chunk).start()
        return 0

    def start_long(chunk, _):
        bring(3, lk_hbm, lk, chunk).start()
        bring(4, lq_hbm, lq, chunk).start()
        return 0

    lax.fori_loop(0, chunks, start_short, 0)
    lax.fori_loop(0, chunks, start_long, 0)

    barrier = pltpu.get_barrier_semaphore()

    def greet_ctx(step, _):
        other = lax.rem(my_ctx + step, n_ctx)
        pl.semaphore_signal(
            barrier, inc=1, device_id={"ctx": other}, device_id_type=pl.DeviceIdType.MESH
        )
        return 0

    def greet_tp(step, _):
        other = lax.rem(my_tp + step, n_tp)
        pl.semaphore_signal(
            barrier, inc=1, device_id={"tp": other}, device_id_type=pl.DeviceIdType.MESH
        )
        return 0

    lax.fori_loop(1, n_ctx, greet_ctx, 0)
    lax.fori_loop(1, n_tp, greet_tp, 0)
    pl.semaphore_wait(barrier, n_ctx + n_tp - 2)

    edge_in(0, sk_hbm, key_edge).wait()
    edge_in(1, sv_hbm, value_edge).wait()
    edge_send[...] = (key_edge[...].astype(F32) * value_edge[...].astype(F32)).astype(BF16)
    edge_copy = pltpu.make_async_remote_copy(
        src_ref=edge_send,
        dst_ref=edge_recv,
        send_sem=edge_sem.at[0],
        recv_sem=edge_sem.at[1],
        device_id={"ctx": lax.rem(my_ctx + 1, n_ctx)},
        device_id_type=pl.DeviceIdType.MESH,
    )
    edge_copy.start()

    row_id = lax.broadcasted_iota(jnp.int32, (block, block), 0)
    col_id = lax.broadcasted_iota(jnp.int32, (block, block), 1)
    lower_mask = jnp.where(col_id >= row_id, 1.0, 0.0).astype(BF16)
    upper_mask = jnp.where(col_id < row_id, 1.0, 0.0).astype(BF16)
    pick_row = lax.broadcasted_iota(jnp.int32, (16, block), 0) % SUB
    row_masks = [jnp.where(pick_row == c, 1.0, 0.0).astype(BF16) for c in range(SUB)]
    sub_id = lax.broadcasted_iota(jnp.int32, (SUB, block), 0)
    lane_id = lax.broadcasted_iota(jnp.int32, (SUB, block), 1)
    own_modes = (lane_id // (block // SUB)) == sub_id

    def spread(stacked):
        rows = stacked.shape[0]
        tiled = stacked.reshape(rows // 16, 16, block)
        return jnp.concatenate(
            [(tiled * row_masks[c][None]).reshape(rows, block) for c in range(SUB)], axis=1
        )

    def circulant(row):
        base = jnp.broadcast_to(row, (16, block))
        base = pltpu.roll(base, 0, 1, stride=1, stride_axis=0).astype(BF16)
        turned = [base] + [pltpu.roll(base, 16 * a, 1) for a in range(1, block // 16)]
        return jnp.concatenate(turned, axis=0)

    def parts(value):
        high = value.astype(BF16)
        return high, (value - high.astype(F32)).astype(BF16)

    def run_pairs(chunk, body):
        lax.fori_loop(
            0, pairs, lambda i, _: body(chunk * pairs + i, 0), 0, unroll=min(2, pairs)
        )

    def at(b):
        return slice(b * block, (b + 1) * block)

    def over(b):
        return slice(b * SUB, (b + 1) * SUB)

    step_at = col_id.astype(F32)
    modes = block // SUB

    def make_params(step, _):
        for g in [step * 4 + i for i in range(4)]:
            decay = jnp.broadcast_to(decay_ref[pl.ds(g, 1), :], (block, block)).T
            weight = jnp.broadcast_to(weight_ref[pl.ds(g, 1), :], (block, block)).T
            tail = jnp.concatenate(parts(jnp.exp(-decay * (block - 1 - step_at))), axis=1)
            kernel = weight * jnp.exp(-decay * step_at)
            high, low = parts(weight * jnp.exp(-decay * (step_at + 1.0)))
            band = []
            for c in range(SUB):
                row = jnp.sum(kernel[c * modes : (c + 1) * modes], axis=0, keepdims=True)
                band.append(circulant(row) * lower_mask)
            tails[g] = tail
            heads[g] = jnp.concatenate([high, high, low], axis=0)
            bands[g] = jnp.concatenate(band, axis=0)
        return 0

    lax.fori_loop(0, groups // 8, make_params, 0)

    squares[...] = jnp.zeros_like(squares)
    edge_copy.wait()
    has_left = jnp.where(my_ctx > 0, 1.0, 0.0).astype(F32)

    def short_pair(pair, _):
        rows = pl.ds(pl.multiple_of(pair * 16, 16), 16)
        product = sk[rows, :].astype(F32) * sv[rows, :].astype(F32)
        query = sq[rows, :].astype(F32)
        edge = edge_recv[rows, :].astype(F32) * has_left
        taps = taps_ref[rows, :].astype(F32)
        gates = []
        for half in range(2):
            own = slice(half * SUB, (half + 1) * SUB)
            stacked = jnp.concatenate(
                [edge[own]]
                + [product[own, at(b)] for b in range(blocks)]
                + [jnp.zeros((SUB, block), F32)],
                axis=0,
            ).astype(BF16)
            bands_now = []
            for c in range(SUB):
                turned = circulant(taps[half * SUB + c : half * SUB + c + 1])
                bands_now.append(
                    jnp.concatenate([turned * lower_mask, turned * upper_mask], axis=1)
                )
            mixed = jnp.dot(
                spread(stacked),
                jnp.concatenate(bands_now, axis=0),
                preferred_element_type=F32,
            )
            gates.append(
                [
                    query[own, at(b)] * (mixed[over(b + 1), :block] + mixed[over(b), block:])
                    for b in range(blocks)
                ]
            )
        for b in range(blocks):
            first, second = gates[0][b], gates[1][b]
            gated[rows, at(b)] = jnp.concatenate([first, second], axis=0)
            squares[:, at(b)] += first * first + second * second
        return 0

    def short_chunk(chunk, _):
        bring(0, sk_hbm, sk, chunk).wait()
        bring(1, sv_hbm, sv, chunk).wait()
        bring(2, sq_hbm, sq, chunk).wait()
        run_pairs(chunk, short_pair)
        return 0

    lax.fori_loop(0, chunks, short_chunk, 0)

    sums[my_tp] = jnp.sum(squares[...], axis=0, keepdims=True)

    def sum_copy(slot, other):
        return pltpu.make_async_remote_copy(
            src_ref=sums.at[slot],
            dst_ref=sums.at[slot],
            send_sem=sum_send_sem.at[other],
            recv_sem=sum_recv_sem.at[slot],
            device_id={"tp": other},
            device_id_type=pl.DeviceIdType.MESH,
        )

    def sum_start(step, _):
        sum_copy(my_tp, lax.rem(my_tp + step, n_tp)).start()
        return 0

    lax.fori_loop(1, n_tp, sum_start, 0)

    lax.fori_loop(groups // 8, groups // 4, make_params, 0)

    def sum_wait(step, _):
        other = lax.rem(my_tp + step, n_tp)
        sum_copy(my_tp, other).wait_send()
        sum_copy(other, other).wait_recv()
        return 0

    lax.fori_loop(1, n_tp, sum_wait, 0)
    total = sums[0]
    for other in range(1, n_tp):
        total = total + sums[other]
    squares[...] = jnp.broadcast_to(lax.rsqrt(total / width + 1e-06), squares.shape)

    def state_pair(pair, _):
        rows = pl.ds(pl.multiple_of(pair * 16, 16), 16)
        key = lk[rows, :].astype(F32)
        for half in range(2):
            own = slice(half * SUB, (half + 1) * SUB)
            g = pair * 2 + half
            place = pl.ds(pl.multiple_of(pair * 16 + half * SUB, SUB), SUB)
            gain = gain_ref[place, :]
            stacked = jnp.concatenate(
                [
                    key[own, at(b)] * (gated[place, at(b)] * gain * squares[:, at(b)])
                    for b in range(blocks)
                ],
                axis=0,
            ).astype(BF16)
            signal[g] = stacked
            ends = lax.dot_general(
                jnp.concatenate([stacked, stacked], axis=1),
                tails[g],
                (((1,), (1,)), ((), ())),
                preferred_element_type=F32,
            )
            fade = jnp.exp(-decay_ref[pl.ds(g, 1), :] * block)
            state = jnp.zeros((SUB, block), F32)
            for b in range(blocks):
                carry[g, over(b), :] = state
                state = fade * state + jnp.where(own_modes, ends[over(b)], 0.0)
            states[my_ctx, pl.ds(g, 1), :] = jnp.sum(state, axis=0, keepdims=True)
        return 0

    def state_chunk(chunk, _):
        bring(3, lk_hbm, lk, chunk).wait()
        run_pairs(chunk, state_pair)
        return 0

    lax.fori_loop(0, chunks, state_chunk, 0)

    def state_copy(slot, other):
        return pltpu.make_async_remote_copy(
            src_ref=states.at[slot],
            dst_ref=states.at[slot],
            send_sem=state_send_sem.at[other],
            recv_sem=state_recv_sem.at[slot],
            device_id={"ctx": other},
            device_id_type=pl.DeviceIdType.MESH,
        )

    def state_start(step, _):
        state_copy(my_ctx, lax.rem(my_ctx + step, n_ctx)).start()
        return 0

    lax.fori_loop(1, n_ctx, state_start, 0)

    def inner_groups(step, _):
        inners = [
            jnp.dot(spread(signal[step * 4 + i]), bands[step * 4 + i], preferred_element_type=F32)
            for i in range(4)
        ]
        rows = pl.ds(pl.multiple_of(step * 4 * SUB, 4 * SUB), 4 * SUB)
        for b in range(blocks):
            gated[rows, at(b)] = jnp.concatenate([inner[over(b)] for inner in inners], axis=0)
        return 0

    lax.fori_loop(0, groups // 4, inner_groups, 0)

    def state_wait(step, _):
        other = lax.rem(my_ctx + step, n_ctx)
        state_copy(my_ctx, other).wait_send()
        state_copy(other, other).wait_recv()
        return 0

    lax.fori_loop(1, n_ctx, state_wait, 0)

    entering = jnp.zeros(decay_ref.shape, F32)
    device_fade = jnp.exp(-decay_ref[...] * length)
    for other in range(n_ctx - 1):
        further = device_fade * entering + states[other]
        entering = jnp.where(other < my_ctx, further, entering)
    states[0] = entering

    def out_copy(chunk):
        rows = pl.ds(pl.multiple_of(chunk * chunk_rows, 16), chunk_rows)
        return pltpu.make_async_copy(gated.at[rows], out_hbm.at[rows], out_sem.at[chunk])

    def last_pair(pair, _):
        rows = pl.ds(pl.multiple_of(pair * 16, 16), 16)
        query = lq[rows, :].astype(F32)
        for half in range(2):
            own = slice(half * SUB, (half + 1) * SUB)
            g = pair * 2 + half
            place = pl.ds(pl.multiple_of(pair * 16 + half * SUB, SUB), SUB)
            fade = jnp.exp(-decay_ref[pl.ds(g, 1), :] * block)
            here = jnp.where(own_modes, states[0, pl.ds(g, 1), :], 0.0)
            before = []
            for b in range(blocks):
                before.append(carry[g, over(b), :] + here)
                here = here * fade
            high, low = parts(jnp.concatenate(before, axis=0))
            carried = jnp.dot(
                jnp.concatenate([high, low, high], axis=1),
                heads[g],
                preferred_element_type=F32,
            )
            for b in range(blocks):
                gated[place, at(b)] = query[own, at(b)] * (gated[place, at(b)] + carried[over(b)])
        return 0

    def last_chunk(chunk, _):
        bring(4, lq_hbm, lq, chunk).wait()
        run_pairs(chunk, last_pair)
        out_copy(chunk).start()
        return 0

    lax.fori_loop(0, chunks, last_chunk, 0)

    def out_wait(chunk, _):
        out_copy(chunk).wait()
        return 0

    lax.fori_loop(0, chunks, out_wait, 0)


def shards(
    short_query,
    short_key,
    short_value,
    short_taps,
    norm_gain,
    long_key,
    long_query,
    residues,
    decay_rates,
):
    channels, length = short_value.shape
    block = short_taps.shape[1]
    modes = decay_rates.shape[0]
    groups = channels // SUB
    assert modes * SUB == block
    n_ctx, n_tp = lax.axis_size("ctx"), lax.axis_size("tp")
    chunks = min(8, channels // 16)
    weights = residues * jnp.sqrt(-jnp.expm1(-2.0 * decay_rates))
    decays = decay_rates.T.reshape(groups, block)
    weights = weights.T.reshape(groups, block)
    gains = jnp.broadcast_to(norm_gain[:, None], (channels, block))
    hbm = pl.BlockSpec(memory_space=pl.ANY)
    vmem = pl.BlockSpec(memory_space=pltpu.VMEM)
    dma = pltpu.SemaphoreType.DMA
    return pl.pallas_call(
        functools.partial(fused, n_ctx, n_tp, channels * n_tp),
        out_shape=jax.ShapeDtypeStruct((channels, length), F32),
        in_specs=[hbm] * 5 + [vmem] * 4,
        out_specs=hbm,
        scratch_shapes=[pltpu.VMEM((channels, length), BF16)] * 5
        + [pltpu.VMEM((channels, block), BF16)] * 4
        + [
            pltpu.VMEM((channels, length), F32),
            pltpu.VMEM((SUB, length), F32),
            pltpu.VMEM((n_tp, 1, length), F32),
            pltpu.VMEM((groups, block, block), BF16),
            pltpu.VMEM((groups, block, 2 * block), BF16),
            pltpu.VMEM((groups, 3 * block, block), BF16),
            pltpu.VMEM((groups, SUB * block, block), BF16),
            pltpu.VMEM((groups, block, block), F32),
            pltpu.VMEM((n_ctx, groups, block), F32),
            dma((5, chunks)),
            dma((2,)),
            dma((chunks,)),
            dma((2,)),
            dma((n_tp,)),
            dma((n_tp,)),
            dma((n_ctx,)),
            dma((n_ctx,)),
        ],
        compiler_params=pltpu.CompilerParams(
            collective_id=0, has_side_effects=True, vmem_limit_bytes=56 * 1024 * 1024
        ),
    )(
        short_query,
        short_key,
        short_value,
        long_key,
        long_query,
        short_taps,
        gains,
        decays,
        weights,
    )


def solution(mesh):
    in_specs = (
        P("tp", "ctx"),
        P("tp", "ctx"),
        P("tp", "ctx"),
        P("tp", None),
        P("tp"),
        P("tp", "ctx"),
        P("tp", "ctx"),
        P(None, "tp"),
        P(None, "tp"),
    )
    out_specs = P("tp", "ctx")
    return jax.shard_map(shards, mesh=mesh, in_specs=in_specs, out_specs=out_specs, check_vma=False)
```

```python
import functools

import jax
import jax.numpy as jnp
from jax import lax
from jax.experimental import pallas as pl
from jax.experimental.pallas import tpu as pltpu
from jax.sharding import PartitionSpec as P

F32 = jnp.float32
BF16 = jnp.bfloat16
SUB = 8


def fused(
    n_ctx,
    n_tp,
    width,
    sq_hbm,
    sk_hbm,
    sv_hbm,
    lk_hbm,
    lq_hbm,
    taps_hbm,
    modes_hbm,
    out_hbm,
    taps_ref,
    modes_ref,
    sq,
    sk,
    sv,
    lk,
    lq,
    key_edge,
    value_edge,
    edge_send,
    edge_recv,
    gated,
    squares,
    sums,
    signal,
    tails,
    heads,
    bands,
    carry,
    states,
    in_sem,
    edge_in_sem,
    small_sem,
    out_sem,
    edge_sem,
    sum_send_sem,
    sum_recv_sem,
    state_send_sem,
    state_recv_sem,
):
    channels, length = gated.shape
    block = taps_ref.shape[1]
    blocks = length // block
    groups = channels // SUB
    chunks = in_sem.shape[1]
    chunk_rows = channels // chunks
    pairs = chunk_rows // 16
    my_ctx = lax.axis_index("ctx")
    my_tp = lax.axis_index("tp")

    def edge_in(which, source, target):
        return pltpu.make_async_copy(
            source.at[:, pl.ds(length - block, block)], target, edge_in_sem.at[which]
        )

    def small_in(which, source, target):
        return pltpu.make_async_copy(source, target, small_sem.at[which])

    def bring(which, source, target, chunk):
        rows = pl.ds(pl.multiple_of(chunk * chunk_rows, 16), chunk_rows)
        return pltpu.make_async_copy(source.at[rows], target.at[rows], in_sem.at[which, chunk])

    edge_in(0, sk_hbm, key_edge).start()
    edge_in(1, sv_hbm, value_edge).start()
    small_in(0, taps_hbm, taps_ref).start()
    small_in(1, modes_hbm, modes_ref).start()
    decay_ref, weight_ref = modes_ref.at[0], modes_ref.at[1]

    def start_short(chunk, _):
        bring(0, sk_hbm, sk, chunk).start()
        bring(1, sv_hbm, sv, chunk).start()
        bring(2, sq_hbm, sq, chunk).start()
        return 0

    def start_long(chunk, _):
        bring(3, lk_hbm, lk, chunk).start()
        bring(4, lq_hbm, lq, chunk).start()
        return 0

    lax.fori_loop(0, chunks, start_short, 0)
    lax.fori_loop(0, chunks, start_long, 0)

    barrier = pltpu.get_barrier_semaphore()

    def greet_ctx(step, _):
        other = lax.rem(my_ctx + step, n_ctx)
        pl.semaphore_signal(
            barrier, inc=1, device_id={"ctx": other}, device_id_type=pl.DeviceIdType.MESH
        )
        return 0

    def greet_tp(step, _):
        other = lax.rem(my_tp + step, n_tp)
        pl.semaphore_signal(
            barrier, inc=1, device_id={"tp": other}, device_id_type=pl.DeviceIdType.MESH
        )
        return 0

    lax.fori_loop(1, n_ctx, greet_ctx, 0)
    lax.fori_loop(1, n_tp, greet_tp, 0)
    pl.semaphore_wait(barrier, n_ctx + n_tp - 2)

    edge_in(0, sk_hbm, key_edge).wait()
    edge_in(1, sv_hbm, value_edge).wait()
    edge_send[...] = (key_edge[...].astype(F32) * value_edge[...].astype(F32)).astype(BF16)
    edge_copy = pltpu.make_async_remote_copy(
        src_ref=edge_send,
        dst_ref=edge_recv,
        send_sem=edge_sem.at[0],
        recv_sem=edge_sem.at[1],
        device_id={"ctx": lax.rem(my_ctx + 1, n_ctx)},
        device_id_type=pl.DeviceIdType.MESH,
    )
    edge_copy.start()

    row_id = lax.broadcasted_iota(jnp.int32, (block, block), 0)
    col_id = lax.broadcasted_iota(jnp.int32, (block, block), 1)
    lower_mask = jnp.where(col_id >= row_id, 1.0, 0.0).astype(BF16)
    upper_mask = jnp.where(col_id < row_id, 1.0, 0.0).astype(BF16)
    pick_row = lax.broadcasted_iota(jnp.int32, (16, block), 0) % SUB
    pair_masks = [jnp.where(pick_row // 2 == s, 1.0, 0.0).astype(BF16) for s in range(SUB // 2)]
    sub_id = lax.broadcasted_iota(jnp.int32, (SUB, block), 0)
    lane_id = lax.broadcasted_iota(jnp.int32, (SUB, block), 1)
    own_modes = (lane_id // (block // SUB)) == sub_id

    odd_row = sub_id % 2 == 1

    def spread(*stacks):
        rows = stacks[0].shape[0]
        return jnp.concatenate(
            [
                (stacked.reshape(rows // 16, 16, block) * pair_masks[s][None]).reshape(rows, block)
                for s in range(SUB // 2)
                for stacked in stacks
            ],
            axis=1,
        )

    def beside(left, right):
        return jnp.concatenate([left, right], axis=1)

    def own_half(mixed, b):
        return jnp.where(odd_row, mixed[over(b), block:], mixed[over(b), :block])

    def circulant(row):
        base = jnp.broadcast_to(row, (16, block))
        base = pltpu.roll(base, 0, 1, stride=1, stride_axis=0).astype(BF16)
        turned = [base] + [pltpu.roll(base, 16 * a, 1) for a in range(1, block // 16)]
        return jnp.concatenate(turned, axis=0)

    def parts(value):
        high = value.astype(BF16)
        return high, (value - high.astype(F32)).astype(BF16)

    def run_pairs(chunk, body):
        lax.fori_loop(
            0, pairs, lambda i, _: body(chunk * pairs + i, 0), 0, unroll=min(2, pairs)
        )

    def at(b):
        return slice(b * block, (b + 1) * block)

    def over(b):
        return slice(b * SUB, (b + 1) * SUB)

    step_at = col_id.astype(F32)

    def make_params(step, _):
        for g in [step * 4 + i for i in range(4)]:
            decay = jnp.broadcast_to(decay_ref[pl.ds(g, 1), :], (block, block)).T
            tail = beside(*parts(jnp.exp(-decay * (block - 1 - step_at))))
            head = beside(*parts(jnp.exp(-decay * step_at)))
            weight = jnp.where(own_modes, weight_ref[pl.ds(g, 1), :], 0.0)
            sums_two = jnp.dot(
                beside(*parts(weight)),
                jnp.concatenate([head, head], axis=0),
                preferred_element_type=F32,
            )
            kernel = sums_two[:, :block] + sums_two[:, block:]
            band = [circulant(kernel[c : c + 1]) * lower_mask for c in range(SUB)]
            tails[g] = tail
            heads[g] = head
            for s in range(SUB // 2):
                bands[g, s * block : (s + 1) * block, :] = beside(band[2 * s], band[2 * s + 1])
        return 0

    small_in(0, taps_hbm, taps_ref).wait()
    small_in(1, modes_hbm, modes_ref).wait()
    lax.fori_loop(0, groups // 8, make_params, 0)

    squares[...] = jnp.zeros_like(squares)
    edge_copy.wait()
    has_left = jnp.where(my_ctx > 0, 1.0, 0.0).astype(F32)

    def short_pair(pair, _):
        rows = pl.ds(pl.multiple_of(pair * 16, 16), 16)
        product = sk[rows, :].astype(F32) * sv[rows, :].astype(F32)
        query = sq[rows, :].astype(F32)
        edge = edge_recv[rows, :].astype(F32) * has_left
        taps = taps_ref[rows, :].astype(F32)
        gates = []
        for half in range(2):
            own = slice(half * SUB, (half + 1) * SUB)
            tiles = [edge[own]] + [product[own, at(b)] for b in range(blocks)]
            before = jnp.concatenate(tiles[:-1], axis=0).astype(BF16)
            current = jnp.concatenate(tiles[1:], axis=0).astype(BF16)
            turned = [circulant(taps[half * SUB + c : half * SUB + c + 1]) for c in range(SUB)]
            bands_now = []
            for s in range(SUB // 2):
                first, second = turned[2 * s], turned[2 * s + 1]
                bands_now.append(beside(first * lower_mask, second * lower_mask))
                bands_now.append(beside(first * upper_mask, second * upper_mask))
            mixed = jnp.dot(
                spread(current, before),
                jnp.concatenate(bands_now, axis=0),
                preferred_element_type=F32,
            )
            gates.append(
                [
                    query[own, at(b)] * own_half(mixed, b)
                    for b in range(blocks)
                ]
            )
        for b in range(blocks):
            first, second = gates[0][b], gates[1][b]
            gated[rows, at(b)] = jnp.concatenate([first, second], axis=0)
            squares[:, at(b)] += first * first + second * second
        return 0

    def short_chunk(chunk, _):
        bring(0, sk_hbm, sk, chunk).wait()
        bring(1, sv_hbm, sv, chunk).wait()
        bring(2, sq_hbm, sq, chunk).wait()
        run_pairs(chunk, short_pair)
        return 0

    lax.fori_loop(0, chunks, short_chunk, 0)

    sums[my_tp] = jnp.sum(squares[...], axis=0, keepdims=True)

    def sum_copy(slot, other):
        return pltpu.make_async_remote_copy(
            src_ref=sums.at[slot],
            dst_ref=sums.at[slot],
            send_sem=sum_send_sem.at[other],
            recv_sem=sum_recv_sem.at[slot],
            device_id={"tp": other},
            device_id_type=pl.DeviceIdType.MESH,
        )

    def sum_start(step, _):
        sum_copy(my_tp, lax.rem(my_tp + step, n_tp)).start()
        return 0

    lax.fori_loop(1, n_tp, sum_start, 0)

    lax.fori_loop(groups // 8, groups // 4, make_params, 0)

    def sum_wait(step, _):
        other = lax.rem(my_tp + step, n_tp)
        sum_copy(my_tp, other).wait_send()
        sum_copy(other, other).wait_recv()
        return 0

    lax.fori_loop(1, n_tp, sum_wait, 0)
    total = sums[0]
    for other in range(1, n_tp):
        total = total + sums[other]
    squares[...] = jnp.broadcast_to(lax.rsqrt(total / width + 1e-06), squares.shape)

    def state_pair(pair, _):
        rows = pl.ds(pl.multiple_of(pair * 16, 16), 16)
        key = lk[rows, :].astype(F32)
        for half in range(2):
            own = slice(half * SUB, (half + 1) * SUB)
            g = pair * 2 + half
            place = pl.ds(pl.multiple_of(pair * 16 + half * SUB, SUB), SUB)
            stacked = jnp.concatenate(
                [
                    key[own, at(b)] * (gated[place, at(b)] * squares[:, at(b)])
                    for b in range(blocks)
                ],
                axis=0,
            ).astype(BF16)
            signal[g] = stacked
            ends = lax.dot_general(
                jnp.concatenate([stacked, stacked], axis=1),
                tails[g],
                (((1,), (1,)), ((), ())),
                preferred_element_type=F32,
            )
            fade = jnp.exp(-decay_ref[pl.ds(g, 1), :] * block)
            state = jnp.zeros((SUB, block), F32)
            for b in range(blocks):
                carry[g, over(b), :] = state
                state = fade * state + jnp.where(own_modes, ends[over(b)], 0.0)
            states[my_ctx, pl.ds(g, 1), :] = jnp.sum(state, axis=0, keepdims=True)
        return 0

    def state_chunk(chunk, _):
        bring(3, lk_hbm, lk, chunk).wait()
        run_pairs(chunk, state_pair)
        return 0

    lax.fori_loop(0, chunks, state_chunk, 0)

    def state_copy(slot, other):
        return pltpu.make_async_remote_copy(
            src_ref=states.at[slot],
            dst_ref=states.at[slot],
            send_sem=state_send_sem.at[other],
            recv_sem=state_recv_sem.at[slot],
            device_id={"ctx": other},
            device_id_type=pl.DeviceIdType.MESH,
        )

    def state_start(step, _):
        state_copy(my_ctx, lax.rem(my_ctx + step, n_ctx)).start()
        return 0

    lax.fori_loop(1, n_ctx, state_start, 0)

    def inner_groups(step, _):
        inners = [
            jnp.dot(spread(signal[step * 4 + i]), bands[step * 4 + i], preferred_element_type=F32)
            for i in range(4)
        ]
        rows = pl.ds(pl.multiple_of(step * 4 * SUB, 4 * SUB), 4 * SUB)
        for b in range(blocks):
            gated[rows, at(b)] = jnp.concatenate(
                [own_half(inner, b) for inner in inners], axis=0
            )
        return 0

    lax.fori_loop(0, groups // 4, inner_groups, 0)

    def state_wait(step, _):
        other = lax.rem(my_ctx + step, n_ctx)
        state_copy(my_ctx, other).wait_send()
        state_copy(other, other).wait_recv()
        return 0

    lax.fori_loop(1, n_ctx, state_wait, 0)

    entering = jnp.zeros(decay_ref.shape, F32)
    device_fade = jnp.exp(-decay_ref[...] * length)
    for other in range(n_ctx - 1):
        further = device_fade * entering + states[other]
        entering = jnp.where(other < my_ctx, further, entering)
    states[0] = entering

    def out_copy(chunk):
        rows = pl.ds(pl.multiple_of(chunk * chunk_rows, 16), chunk_rows)
        return pltpu.make_async_copy(gated.at[rows], out_hbm.at[rows], out_sem.at[chunk])

    def last_pair(pair, _):
        rows = pl.ds(pl.multiple_of(pair * 16, 16), 16)
        query = lq[rows, :].astype(F32)
        for half in range(2):
            own = slice(half * SUB, (half + 1) * SUB)
            g = pair * 2 + half
            place = pl.ds(pl.multiple_of(pair * 16 + half * SUB, SUB), SUB)
            fade = jnp.exp(-decay_ref[pl.ds(g, 1), :] * block)
            here = jnp.where(own_modes, states[0, pl.ds(g, 1), :], 0.0)
            before = []
            for b in range(blocks):
                before.append(carry[g, over(b), :] + here)
                here = here * fade
            scale = weight_ref[pl.ds(g, 1), :] * jnp.exp(-decay_ref[pl.ds(g, 1), :])
            carried = jnp.dot(
                beside(*parts(jnp.concatenate(before, axis=0) * scale)),
                jnp.concatenate([heads[g], heads[g]], axis=0),
                preferred_element_type=F32,
            )
            carried = carried[:, :block] + carried[:, block:]
            for b in range(blocks):
                gated[place, at(b)] = query[own, at(b)] * (gated[place, at(b)] + carried[over(b)])
        return 0

    def last_chunk(chunk, _):
        bring(4, lq_hbm, lq, chunk).wait()
        run_pairs(chunk, last_pair)
        out_copy(chunk).start()
        return 0

    lax.fori_loop(0, chunks, last_chunk, 0)

    def out_wait(chunk, _):
        out_copy(chunk).wait()
        return 0

    lax.fori_loop(0, chunks, out_wait, 0)


def shards(
    short_query,
    short_key,
    short_value,
    short_taps,
    norm_gain,
    long_key,
    long_query,
    residues,
    decay_rates,
):
    channels, length = short_value.shape
    block = short_taps.shape[1]
    modes = decay_rates.shape[0]
    groups = channels // SUB
    assert modes * SUB == block
    n_ctx, n_tp = lax.axis_size("ctx"), lax.axis_size("tp")
    chunks = min(8, channels // 16)
    weights = residues * jnp.sqrt(-jnp.expm1(-2.0 * decay_rates)) * norm_gain[None, :]
    both = jnp.stack([decay_rates, weights]).transpose(0, 2, 1).reshape(2, groups, block)
    hbm = pl.BlockSpec(memory_space=pl.ANY)
    dma = pltpu.SemaphoreType.DMA
    return pl.pallas_call(
        functools.partial(fused, n_ctx, n_tp, channels * n_tp),
        out_shape=jax.ShapeDtypeStruct((channels, length), F32),
        in_specs=[hbm] * 7,
        out_specs=hbm,
        scratch_shapes=[
            pltpu.VMEM((channels, block), BF16),
            pltpu.VMEM((2, groups, block), F32),
        ]
        + [pltpu.VMEM((channels, length), BF16)] * 5
        + [pltpu.VMEM((channels, block), BF16)] * 4
        + [
            pltpu.VMEM((channels, length), F32),
            pltpu.VMEM((SUB, length), F32),
            pltpu.VMEM((n_tp, 1, length), F32),
            pltpu.VMEM((groups, block, block), BF16),
            pltpu.VMEM((groups, block, 2 * block), BF16),
            pltpu.VMEM((groups, block, 2 * block), BF16),
            pltpu.VMEM((groups, SUB // 2 * block, 2 * block), BF16),
            pltpu.VMEM((groups, block, block), F32),
            pltpu.VMEM((n_ctx, groups, block), F32),
            dma((5, chunks)),
            dma((2,)),
            dma((2,)),
            dma((chunks,)),
            dma((2,)),
            dma((n_tp,)),
            dma((n_tp,)),
            dma((n_ctx,)),
            dma((n_ctx,)),
        ],
        compiler_params=pltpu.CompilerParams(
            collective_id=0, has_side_effects=True, vmem_limit_bytes=56 * 1024 * 1024
        ),
    )(
        short_query,
        short_key,
        short_value,
        long_key,
        long_query,
        short_taps,
        both,
    )


def solution(mesh):
    in_specs = (
        P("tp", "ctx"),
        P("tp", "ctx"),
        P("tp", "ctx"),
        P("tp", None),
        P("tp"),
        P("tp", "ctx"),
        P("tp", "ctx"),
        P(None, "tp"),
        P(None, "tp"),
    )
    out_specs = P("tp", "ctx")
    return jax.shard_map(shards, mesh=mesh, in_specs=in_specs, out_specs=out_specs, check_vma=False)
```

```python
import functools

import jax
import jax.numpy as jnp
from jax import lax
from jax.experimental import pallas as pl
from jax.experimental.pallas import tpu as pltpu
from jax.sharding import PartitionSpec as P

F32 = jnp.float32
BF16 = jnp.bfloat16
SUB = 8


def fused(
    n_ctx,
    n_tp,
    width,
    sq_hbm,
    sk_hbm,
    sv_hbm,
    lk_hbm,
    lq_hbm,
    taps_hbm,
    modes_hbm,
    out_hbm,
    taps_ref,
    modes_ref,
    sq,
    sk,
    sv,
    lk,
    lq,
    key_edge,
    value_edge,
    edge_send,
    edge_recv,
    gated,
    squares,
    sums,
    signal,
    tails,
    heads,
    bands,
    carry,
    inner,
    turn_in,
    turn_out,
    states,
    in_sem,
    edge_in_sem,
    small_sem,
    out_sem,
    edge_sem,
    sum_send_sem,
    sum_recv_sem,
    state_send_sem,
    state_recv_sem,
):
    channels, length = gated.shape
    block = taps_ref.shape[1]
    blocks = length // block
    groups = channels // SUB
    chunks = in_sem.shape[1]
    chunk_rows = channels // chunks
    pairs = chunk_rows // 16
    per = min(2, pairs)
    my_ctx = lax.axis_index("ctx")
    my_tp = lax.axis_index("tp")

    def edge_in(which, source, target):
        return pltpu.make_async_copy(
            source.at[:, pl.ds(length - block, block)], target, edge_in_sem.at[which]
        )

    def small_in(which, source, target):
        return pltpu.make_async_copy(source, target, small_sem.at[which])

    def bring(which, source, target, chunk):
        rows = pl.ds(pl.multiple_of(chunk * chunk_rows, 16), chunk_rows)
        return pltpu.make_async_copy(source.at[rows], target.at[rows], in_sem.at[which, chunk])

    edge_in(0, sk_hbm, key_edge).start()
    edge_in(1, sv_hbm, value_edge).start()
    small_in(0, taps_hbm, taps_ref).start()
    small_in(1, modes_hbm, modes_ref).start()
    decay_ref, weight_ref = modes_ref.at[0], modes_ref.at[1]

    def start_short(chunk, _):
        bring(0, sk_hbm, sk, chunk).start()
        bring(1, sv_hbm, sv, chunk).start()
        bring(2, sq_hbm, sq, chunk).start()
        return 0

    def start_long(chunk, _):
        bring(3, lk_hbm, lk, chunk).start()
        bring(4, lq_hbm, lq, chunk).start()
        return 0

    lax.fori_loop(0, chunks, start_short, 0)
    lax.fori_loop(0, chunks, start_long, 0)

    barrier = pltpu.get_barrier_semaphore()

    def greet_ctx(step, _):
        other = lax.rem(my_ctx + step, n_ctx)
        pl.semaphore_signal(
            barrier, inc=1, device_id={"ctx": other}, device_id_type=pl.DeviceIdType.MESH
        )
        return 0

    def greet_tp(step, _):
        other = lax.rem(my_tp + step, n_tp)
        pl.semaphore_signal(
            barrier, inc=1, device_id={"tp": other}, device_id_type=pl.DeviceIdType.MESH
        )
        return 0

    lax.fori_loop(1, n_ctx, greet_ctx, 0)
    lax.fori_loop(1, n_tp, greet_tp, 0)
    pl.semaphore_wait(barrier, n_ctx + n_tp - 2)

    edge_in(0, sk_hbm, key_edge).wait()
    edge_in(1, sv_hbm, value_edge).wait()
    edge_send[...] = (key_edge[...].astype(F32) * value_edge[...].astype(F32)).astype(BF16)
    edge_copy = pltpu.make_async_remote_copy(
        src_ref=edge_send,
        dst_ref=edge_recv,
        send_sem=edge_sem.at[0],
        recv_sem=edge_sem.at[1],
        device_id={"ctx": lax.rem(my_ctx + 1, n_ctx)},
        device_id_type=pl.DeviceIdType.MESH,
    )
    edge_copy.start()

    row_id = lax.broadcasted_iota(jnp.int32, (block, block), 0)
    col_id = lax.broadcasted_iota(jnp.int32, (block, block), 1)
    lower_mask = jnp.where(col_id >= row_id, 1.0, 0.0).astype(BF16)
    upper_mask = jnp.where(col_id < row_id, 1.0, 0.0).astype(BF16)
    sub_id = lax.broadcasted_iota(jnp.int32, (SUB, block), 0)
    lane_id = lax.broadcasted_iota(jnp.int32, (SUB, block), 1)
    own_modes = (lane_id // (block // SUB)) == sub_id

    def beside(left, right):
        return jnp.concatenate([left, right], axis=1)

    def channel_rows(first):
        return pl.ds(first, blocks, stride=SUB)

    def circulant(row):
        base = jnp.broadcast_to(row, (16, block))
        base = pltpu.roll(base, 0, 1, stride=1, stride_axis=0).astype(BF16)
        turned = [base] + [pltpu.roll(base, 16 * a, 1) for a in range(1, block // 16)]
        return jnp.concatenate(turned, axis=0)

    def parts(value):
        high = value.astype(BF16)
        return high, (value - high.astype(F32)).astype(BF16)

    def run_pairs(chunk, body):
        def step(i, _):
            body([chunk * pairs + i * per + k for k in range(per)])
            return 0

        lax.fori_loop(0, pairs // per, step, 0)

    def at(b):
        return slice(b * block, (b + 1) * block)

    def over(b):
        return slice(b * SUB, (b + 1) * SUB)

    step_at = col_id.astype(F32)

    def make_params(step, _):
        for g in [step * 4 + i for i in range(4)]:
            decay = jnp.broadcast_to(decay_ref[pl.ds(g, 1), :], (block, block)).T
            tail = beside(*parts(jnp.exp(-decay * (block - 1 - step_at))))
            head = beside(*parts(jnp.exp(-decay * step_at)))
            weight = jnp.where(own_modes, weight_ref[pl.ds(g, 1), :], 0.0)
            sums_two = jnp.dot(
                beside(*parts(weight)),
                jnp.concatenate([head, head], axis=0),
                preferred_element_type=F32,
            )
            kernel = sums_two[:, :block] + sums_two[:, block:]
            band = [circulant(kernel[c : c + 1]) * lower_mask for c in range(SUB)]
            tails[g] = tail
            heads[g] = head
            for s in range(SUB // 2):
                bands[g, s * block : (s + 1) * block, :] = beside(band[2 * s], band[2 * s + 1])
        return 0

    small_in(0, taps_hbm, taps_ref).wait()
    small_in(1, modes_hbm, modes_ref).wait()
    lax.fori_loop(0, groups // 8, make_params, 0)

    squares[...] = jnp.zeros_like(squares)
    edge_copy.wait()
    has_left = jnp.where(my_ctx > 0, 1.0, 0.0).astype(F32)

    def short_pairs(todo):
        places = [pl.ds(pl.multiple_of(pair * 16, 16), 16) for pair in todo]
        for k, rows in enumerate(places):
            product = sk[rows, :].astype(F32) * sv[rows, :].astype(F32)
            edge = edge_recv[rows, :].astype(F32) * has_left
            for half in range(2):
                own = slice(half * SUB, (half + 1) * SUB)
                turn_in[2 * k + half, over(0), :] = edge[own]
                for b in range(blocks):
                    turn_in[2 * k + half, over(b + 1), :] = product[own, at(b)]
        for k, rows in enumerate(places):
            taps = taps_ref[rows, :].astype(F32)
            for half in range(2):
                slot = 2 * k + half
                for s in range(SUB // 2):
                    windows, bands_now = [], []
                    for c in (2 * s, 2 * s + 1):
                        windows.append(
                            beside(
                                turn_in[slot, channel_rows(SUB + c), :].astype(BF16),
                                turn_in[slot, channel_rows(c), :].astype(BF16),
                            )
                        )
                        turned = circulant(taps[half * SUB + c : half * SUB + c + 1])
                        bands_now.append(
                            jnp.concatenate([turned * lower_mask, turned * upper_mask], axis=0)
                        )
                    mixed = jnp.dot(
                        jnp.concatenate(windows, axis=0),
                        beside(*bands_now),
                        preferred_element_type=F32,
                    )
                    turn_out[slot, channel_rows(2 * s), :] = mixed[:blocks, :block]
                    turn_out[slot, channel_rows(2 * s + 1), :] = mixed[blocks:, block:]
        queries = [sq[rows, :].astype(F32) for rows in places]
        for b in range(blocks):
            square = squares[:, at(b)]
            for k, rows in enumerate(places):
                mix = jnp.concatenate(
                    [turn_out[2 * k, over(b), :], turn_out[2 * k + 1, over(b), :]], axis=0
                )
                gate = queries[k][:, at(b)] * mix
                gated[rows, at(b)] = gate
                square = square + gate[:SUB] * gate[:SUB] + gate[SUB:] * gate[SUB:]
            squares[:, at(b)] = square

    def short_chunk(chunk, _):
        bring(0, sk_hbm, sk, chunk).wait()
        bring(1, sv_hbm, sv, chunk).wait()
        bring(2, sq_hbm, sq, chunk).wait()
        run_pairs(chunk, short_pairs)
        return 0

    lax.fori_loop(0, chunks, short_chunk, 0)

    sums[my_tp] = jnp.sum(squares[...], axis=0, keepdims=True)

    def sum_copy(slot, other):
        return pltpu.make_async_remote_copy(
            src_ref=sums.at[slot],
            dst_ref=sums.at[slot],
            send_sem=sum_send_sem.at[other],
            recv_sem=sum_recv_sem.at[slot],
            device_id={"tp": other},
            device_id_type=pl.DeviceIdType.MESH,
        )

    def sum_start(step, _):
        sum_copy(my_tp, lax.rem(my_tp + step, n_tp)).start()
        return 0

    lax.fori_loop(1, n_tp, sum_start, 0)

    lax.fori_loop(groups // 8, groups // 4, make_params, 0)

    def sum_wait(step, _):
        other = lax.rem(my_tp + step, n_tp)
        sum_copy(my_tp, other).wait_send()
        sum_copy(other, other).wait_recv()
        return 0

    lax.fori_loop(1, n_tp, sum_wait, 0)
    total = sums[0]
    for other in range(1, n_tp):
        total = total + sums[other]
    squares[...] = jnp.broadcast_to(lax.rsqrt(total / width + 1e-06), squares.shape)

    def state_pair(pair, k):
        rows = pl.ds(pl.multiple_of(pair * 16, 16), 16)
        key = lk[rows, :].astype(F32)
        for half in range(2):
            own = slice(half * SUB, (half + 1) * SUB)
            g = pair * 2 + half
            place = pl.ds(pl.multiple_of(pair * 16 + half * SUB, SUB), SUB)
            whole = jnp.concatenate(
                [
                    key[own, at(b)] * (gated[place, at(b)] * squares[:, at(b)])
                    for b in range(blocks)
                ],
                axis=0,
            )
            stacked = whole.astype(BF16)
            turn_out[2 * k + half] = whole
            signal[g] = jnp.concatenate(
                [turn_out[2 * k + half, channel_rows(c), :] for c in range(SUB)], axis=0
            ).astype(BF16)
            ends = lax.dot_general(
                jnp.concatenate([stacked, stacked], axis=1),
                tails[g],
                (((1,), (1,)), ((), ())),
                preferred_element_type=F32,
            )
            fade = jnp.exp(-decay_ref[pl.ds(g, 1), :] * block)
            state = jnp.zeros((SUB, block), F32)
            for b in range(blocks):
                carry[g, over(b), :] = state
                state = fade * state + jnp.where(own_modes, ends[over(b)], 0.0)
            states[my_ctx, pl.ds(g, 1), :] = jnp.sum(state, axis=0, keepdims=True)

    def state_pairs(todo):
        for k, pair in enumerate(todo):
            state_pair(pair, k)

    def state_chunk(chunk, _):
        bring(3, lk_hbm, lk, chunk).wait()
        run_pairs(chunk, state_pairs)
        return 0

    lax.fori_loop(0, chunks, state_chunk, 0)

    def state_copy(slot, other):
        return pltpu.make_async_remote_copy(
            src_ref=states.at[slot],
            dst_ref=states.at[slot],
            send_sem=state_send_sem.at[other],
            recv_sem=state_recv_sem.at[slot],
            device_id={"ctx": other},
            device_id_type=pl.DeviceIdType.MESH,
        )

    def state_start(step, _):
        state_copy(my_ctx, lax.rem(my_ctx + step, n_ctx)).start()
        return 0

    lax.fori_loop(1, n_ctx, state_start, 0)

    def inner_groups(step, _):
        for g in [step * 4 + i for i in range(4)]:
            rows = signal[g]
            for q in range(SUB // 4):
                half = 2 * blocks
                first = rows[2 * q * half : (2 * q + 1) * half]
                second = rows[(2 * q + 1) * half : (2 * q + 2) * half]
                empty = jnp.zeros_like(first)
                mixed = jnp.dot(
                    jnp.concatenate([beside(first, empty), beside(empty, second)], axis=0),
                    bands[g, 2 * q * block : (2 * q + 2) * block, :],
                    preferred_element_type=F32,
                )
                for c in range(4):
                    side = slice((c % 2) * block, (c % 2 + 1) * block)
                    inner[g, channel_rows(4 * q + c), :] = mixed[
                        c * blocks : (c + 1) * blocks, side
                    ]
        return 0

    lax.fori_loop(0, groups // 4, inner_groups, 0)

    def state_wait(step, _):
        other = lax.rem(my_ctx + step, n_ctx)
        state_copy(my_ctx, other).wait_send()
        state_copy(other, other).wait_recv()
        return 0

    lax.fori_loop(1, n_ctx, state_wait, 0)

    entering = jnp.zeros(decay_ref.shape, F32)
    device_fade = jnp.exp(-decay_ref[...] * length)
    for other in range(n_ctx - 1):
        further = device_fade * entering + states[other]
        entering = jnp.where(other < my_ctx, further, entering)
    states[0] = entering

    def out_copy(chunk):
        rows = pl.ds(pl.multiple_of(chunk * chunk_rows, 16), chunk_rows)
        return pltpu.make_async_copy(gated.at[rows], out_hbm.at[rows], out_sem.at[chunk])

    def last_pair(pair):
        rows = pl.ds(pl.multiple_of(pair * 16, 16), 16)
        query = lq[rows, :].astype(F32)
        for half in range(2):
            own = slice(half * SUB, (half + 1) * SUB)
            g = pair * 2 + half
            place = pl.ds(pl.multiple_of(pair * 16 + half * SUB, SUB), SUB)
            fade = jnp.exp(-decay_ref[pl.ds(g, 1), :] * block)
            here = jnp.where(own_modes, states[0, pl.ds(g, 1), :], 0.0)
            before = []
            for b in range(blocks):
                before.append(carry[g, over(b), :] + here)
                here = here * fade
            scale = weight_ref[pl.ds(g, 1), :] * jnp.exp(-decay_ref[pl.ds(g, 1), :])
            carried = jnp.dot(
                beside(*parts(jnp.concatenate(before, axis=0) * scale)),
                jnp.concatenate([heads[g], heads[g]], axis=0),
                preferred_element_type=F32,
            )
            carried = carried[:, :block] + carried[:, block:]
            for b in range(blocks):
                gated[place, at(b)] = query[own, at(b)] * (inner[g, over(b), :] + carried[over(b)])

    def last_pairs(todo):
        for pair in todo:
            last_pair(pair)

    def last_chunk(chunk, _):
        bring(4, lq_hbm, lq, chunk).wait()
        run_pairs(chunk, last_pairs)
        out_copy(chunk).start()
        return 0

    lax.fori_loop(0, chunks, last_chunk, 0)

    def out_wait(chunk, _):
        out_copy(chunk).wait()
        return 0

    lax.fori_loop(0, chunks, out_wait, 0)


def shards(
    short_query,
    short_key,
    short_value,
    short_taps,
    norm_gain,
    long_key,
    long_query,
    residues,
    decay_rates,
):
    channels, length = short_value.shape
    block = short_taps.shape[1]
    modes = decay_rates.shape[0]
    groups = channels // SUB
    rows = length // block * SUB
    assert modes * SUB == block
    n_ctx, n_tp = lax.axis_size("ctx"), lax.axis_size("tp")
    chunks = min(8, channels // 16)
    weights = residues * jnp.sqrt(-jnp.expm1(-2.0 * decay_rates)) * norm_gain[None, :]
    both = jnp.stack([decay_rates, weights]).transpose(0, 2, 1).reshape(2, groups, block)
    hbm = pl.BlockSpec(memory_space=pl.ANY)
    dma = pltpu.SemaphoreType.DMA
    return pl.pallas_call(
        functools.partial(fused, n_ctx, n_tp, channels * n_tp),
        out_shape=jax.ShapeDtypeStruct((channels, length), F32),
        in_specs=[hbm] * 7,
        out_specs=hbm,
        scratch_shapes=[
            pltpu.VMEM((channels, block), BF16),
            pltpu.VMEM((2, groups, block), F32),
        ]
        + [pltpu.VMEM((channels, length), BF16)] * 5
        + [pltpu.VMEM((channels, block), BF16)] * 4
        + [
            pltpu.VMEM((channels, length), F32),
            pltpu.VMEM((SUB, length), F32),
            pltpu.VMEM((n_tp, 1, length), F32),
            pltpu.VMEM((groups, rows, block), BF16),
            pltpu.VMEM((groups, block, 2 * block), BF16),
            pltpu.VMEM((groups, block, 2 * block), BF16),
            pltpu.VMEM((groups, SUB // 2 * block, 2 * block), BF16),
            pltpu.VMEM((groups, rows, block), F32),
            pltpu.VMEM((groups, rows, block), F32),
            pltpu.VMEM((4, rows + SUB, block), F32),
            pltpu.VMEM((4, rows, block), F32),
            pltpu.VMEM((n_ctx, groups, block), F32),
            dma((5, chunks)),
            dma((2,)),
            dma((2,)),
            dma((chunks,)),
            dma((2,)),
            dma((n_tp,)),
            dma((n_tp,)),
            dma((n_ctx,)),
            dma((n_ctx,)),
        ],
        compiler_params=pltpu.CompilerParams(
            collective_id=0, has_side_effects=True, vmem_limit_bytes=56 * 1024 * 1024
        ),
    )(
        short_query,
        short_key,
        short_value,
        long_key,
        long_query,
        short_taps,
        both,
    )


def solution(mesh):
    in_specs = (
        P("tp", "ctx"),
        P("tp", "ctx"),
        P("tp", "ctx"),
        P("tp", None),
        P("tp"),
        P("tp", "ctx"),
        P("tp", "ctx"),
        P(None, "tp"),
        P(None, "tp"),
    )
    out_specs = P("tp", "ctx")
    return jax.shard_map(shards, mesh=mesh, in_specs=in_specs, out_specs=out_specs, check_vma=False)
```

```python
import functools

import jax
import jax.numpy as jnp
from jax import lax
from jax.experimental import pallas as pl
from jax.experimental.pallas import tpu as pltpu
from jax.sharding import PartitionSpec as P

F32 = jnp.float32
BF16 = jnp.bfloat16
SUB = 8


def fused(
    n_ctx,
    n_tp,
    width,
    sq_hbm,
    sk_hbm,
    sv_hbm,
    lk_hbm,
    lq_hbm,
    taps_hbm,
    modes_hbm,
    out_hbm,
    taps_ref,
    modes_ref,
    sq,
    sk,
    sv,
    lk,
    lq,
    key_edge,
    value_edge,
    edge_send,
    edge_recv,
    gated,
    squares,
    sums,
    signal,
    tails,
    heads,
    bands,
    carry,
    inner,
    turn_in,
    turn_out,
    states,
    in_sem,
    edge_in_sem,
    small_sem,
    out_sem,
    edge_sem,
    sum_send_sem,
    sum_recv_sem,
    state_send_sem,
    state_recv_sem,
):
    channels, length = gated.shape
    block = taps_ref.shape[1]
    blocks = length // block
    groups = channels // SUB
    many = min(8, groups // 2)
    chunks = in_sem.shape[1]
    chunk_rows = channels // chunks
    pairs = chunk_rows // 16
    per = min(4, pairs)
    my_ctx = lax.axis_index("ctx")
    my_tp = lax.axis_index("tp")

    def edge_in(which, source, target):
        return pltpu.make_async_copy(
            source.at[:, pl.ds(length - block, block)], target, edge_in_sem.at[which]
        )

    def small_in(which, source, target):
        return pltpu.make_async_copy(source, target, small_sem.at[which])

    def bring(which, source, target, chunk):
        rows = pl.ds(pl.multiple_of(chunk * chunk_rows, 16), chunk_rows)
        return pltpu.make_async_copy(source.at[rows], target.at[rows], in_sem.at[which, chunk])

    edge_in(0, sk_hbm, key_edge).start()
    edge_in(1, sv_hbm, value_edge).start()
    small_in(0, taps_hbm, taps_ref).start()
    small_in(1, modes_hbm, modes_ref).start()
    decay_ref, weight_ref = modes_ref.at[0], modes_ref.at[1]

    def start_short(chunk, _):
        bring(0, sk_hbm, sk, chunk).start()
        bring(1, sv_hbm, sv, chunk).start()
        bring(2, sq_hbm, sq, chunk).start()
        return 0

    def start_long(chunk, _):
        bring(3, lk_hbm, lk, chunk).start()
        bring(4, lq_hbm, lq, chunk).start()
        return 0

    lax.fori_loop(0, chunks, start_short, 0)
    lax.fori_loop(0, chunks, start_long, 0)

    barrier = pltpu.get_barrier_semaphore()

    def greet_ctx(step, _):
        other = lax.rem(my_ctx + step, n_ctx)
        pl.semaphore_signal(
            barrier, inc=1, device_id={"ctx": other}, device_id_type=pl.DeviceIdType.MESH
        )
        return 0

    def greet_tp(step, _):
        other = lax.rem(my_tp + step, n_tp)
        pl.semaphore_signal(
            barrier, inc=1, device_id={"tp": other}, device_id_type=pl.DeviceIdType.MESH
        )
        return 0

    lax.fori_loop(1, n_ctx, greet_ctx, 0)
    lax.fori_loop(1, n_tp, greet_tp, 0)
    pl.semaphore_wait(barrier, n_ctx + n_tp - 2)

    edge_in(0, sk_hbm, key_edge).wait()
    edge_in(1, sv_hbm, value_edge).wait()
    edge_send[...] = (key_edge[...].astype(F32) * value_edge[...].astype(F32)).astype(BF16)
    edge_copy = pltpu.make_async_remote_copy(
        src_ref=edge_send,
        dst_ref=edge_recv,
        send_sem=edge_sem.at[0],
        recv_sem=edge_sem.at[1],
        device_id={"ctx": lax.rem(my_ctx + 1, n_ctx)},
        device_id_type=pl.DeviceIdType.MESH,
    )
    edge_copy.start()

    row_id = lax.broadcasted_iota(jnp.int32, (block, block), 0)
    col_id = lax.broadcasted_iota(jnp.int32, (block, block), 1)
    lower_mask = jnp.where(col_id >= row_id, 1.0, 0.0).astype(BF16)
    upper_mask = jnp.where(col_id < row_id, 1.0, 0.0).astype(BF16)
    sub_id = lax.broadcasted_iota(jnp.int32, (SUB, block), 0)
    lane_id = lax.broadcasted_iota(jnp.int32, (SUB, block), 1)
    own_modes = (lane_id // (block // SUB)) == sub_id

    def beside(left, right):
        return jnp.concatenate([left, right], axis=1)

    def channel_rows(first):
        return pl.ds(first, blocks, stride=SUB)

    def circulant(row):
        base = jnp.broadcast_to(row, (16, block))
        base = pltpu.roll(base, 0, 1, stride=1, stride_axis=0).astype(BF16)
        turned = [base] + [pltpu.roll(base, 16 * a, 1) for a in range(1, block // 16)]
        return jnp.concatenate(turned, axis=0)

    def parts(value):
        high = value.astype(BF16)
        return high, (value - high.astype(F32)).astype(BF16)

    def run_pairs(chunk, body):
        def step(i, _):
            body([chunk * pairs + i * per + k for k in range(per)])
            return 0

        lax.fori_loop(0, pairs // per, step, 0)

    def at(b):
        return slice(b * block, (b + 1) * block)

    def over(b):
        return slice(b * SUB, (b + 1) * SUB)

    step_at = col_id.astype(F32)

    def make_params(step, _):
        for g in [step * many + i for i in range(many)]:
            decay = jnp.broadcast_to(decay_ref[pl.ds(g, 1), :], (block, block)).T
            tail = beside(*parts(jnp.exp(-decay * (block - 1 - step_at))))
            head = beside(*parts(jnp.exp(-decay * step_at)))
            weight = jnp.where(own_modes, weight_ref[pl.ds(g, 1), :], 0.0)
            sums_two = jnp.dot(
                beside(*parts(weight)),
                jnp.concatenate([head, head], axis=0),
                preferred_element_type=F32,
            )
            kernel = sums_two[:, :block] + sums_two[:, block:]
            band = [circulant(kernel[c : c + 1]) * lower_mask for c in range(SUB)]
            tails[g] = tail
            heads[g] = head
            for s in range(SUB // 2):
                bands[g, s * block : (s + 1) * block, :] = beside(band[2 * s], band[2 * s + 1])
        return 0

    small_in(0, taps_hbm, taps_ref).wait()
    small_in(1, modes_hbm, modes_ref).wait()
    lax.fori_loop(0, groups // many // 2, make_params, 0)

    squares[...] = jnp.zeros_like(squares)
    edge_copy.wait()
    has_left = jnp.where(my_ctx > 0, 1.0, 0.0).astype(F32)

    def short_pairs(todo):
        places = [pl.ds(pl.multiple_of(pair * 16, 16), 16) for pair in todo]
        for k, rows in enumerate(places):
            product = sk[rows, :].astype(F32) * sv[rows, :].astype(F32)
            edge = edge_recv[rows, :].astype(F32) * has_left
            for half in range(2):
                own = slice(half * SUB, (half + 1) * SUB)
                turn_in[2 * k + half, over(0), :] = edge[own]
                for b in range(blocks):
                    turn_in[2 * k + half, over(b + 1), :] = product[own, at(b)]
        for k, rows in enumerate(places):
            taps = taps_ref[rows, :].astype(F32)
            for half in range(2):
                slot = 2 * k + half
                for s in range(SUB // 2):
                    windows, bands_now = [], []
                    for c in (2 * s, 2 * s + 1):
                        windows.append(
                            beside(
                                turn_in[slot, channel_rows(SUB + c), :].astype(BF16),
                                turn_in[slot, channel_rows(c), :].astype(BF16),
                            )
                        )
                        turned = circulant(taps[half * SUB + c : half * SUB + c + 1])
                        bands_now.append(
                            jnp.concatenate([turned * lower_mask, turned * upper_mask], axis=0)
                        )
                    mixed = jnp.dot(
                        jnp.concatenate(windows, axis=0),
                        beside(*bands_now),
                        preferred_element_type=F32,
                    )
                    turn_out[slot, channel_rows(2 * s), :] = mixed[:blocks, :block]
                    turn_out[slot, channel_rows(2 * s + 1), :] = mixed[blocks:, block:]
        queries = [sq[rows, :].astype(F32) for rows in places]
        for b in range(blocks):
            square = squares[:, at(b)]
            for k, rows in enumerate(places):
                mix = jnp.concatenate(
                    [turn_out[2 * k, over(b), :], turn_out[2 * k + 1, over(b), :]], axis=0
                )
                gate = queries[k][:, at(b)] * mix
                gated[rows, at(b)] = gate
                square = square + gate[:SUB] * gate[:SUB] + gate[SUB:] * gate[SUB:]
            squares[:, at(b)] = square

    def short_chunk(chunk, _):
        bring(0, sk_hbm, sk, chunk).wait()
        bring(1, sv_hbm, sv, chunk).wait()
        bring(2, sq_hbm, sq, chunk).wait()
        run_pairs(chunk, short_pairs)
        return 0

    lax.fori_loop(0, chunks, short_chunk, 0)

    sums[my_tp] = jnp.sum(squares[...], axis=0, keepdims=True)

    def sum_copy(slot, other):
        return pltpu.make_async_remote_copy(
            src_ref=sums.at[slot],
            dst_ref=sums.at[slot],
            send_sem=sum_send_sem.at[other],
            recv_sem=sum_recv_sem.at[slot],
            device_id={"tp": other},
            device_id_type=pl.DeviceIdType.MESH,
        )

    def sum_start(step, _):
        sum_copy(my_tp, lax.rem(my_tp + step, n_tp)).start()
        return 0

    lax.fori_loop(1, n_tp, sum_start, 0)

    lax.fori_loop(groups // many // 2, groups // many, make_params, 0)

    def sum_wait(step, _):
        other = lax.rem(my_tp + step, n_tp)
        sum_copy(my_tp, other).wait_send()
        sum_copy(other, other).wait_recv()
        return 0

    lax.fori_loop(1, n_tp, sum_wait, 0)
    total = sums[0]
    for other in range(1, n_tp):
        total = total + sums[other]
    squares[...] = jnp.broadcast_to(lax.rsqrt(total / width + 1e-06), squares.shape)

    def state_pair(pair, k):
        rows = pl.ds(pl.multiple_of(pair * 16, 16), 16)
        key = lk[rows, :].astype(F32)
        for half in range(2):
            own = slice(half * SUB, (half + 1) * SUB)
            g = pair * 2 + half
            place = pl.ds(pl.multiple_of(pair * 16 + half * SUB, SUB), SUB)
            whole = jnp.concatenate(
                [
                    key[own, at(b)] * (gated[place, at(b)] * squares[:, at(b)])
                    for b in range(blocks)
                ],
                axis=0,
            )
            stacked = whole.astype(BF16)
            turn_out[2 * k + half] = whole
            signal[g] = jnp.concatenate(
                [turn_out[2 * k + half, channel_rows(c), :] for c in range(SUB)], axis=0
            ).astype(BF16)
            ends = lax.dot_general(
                jnp.concatenate([stacked, stacked], axis=1),
                tails[g],
                (((1,), (1,)), ((), ())),
                preferred_element_type=F32,
            )
            fade = jnp.exp(-decay_ref[pl.ds(g, 1), :] * block)
            state = jnp.zeros((SUB, block), F32)
            for b in range(blocks):
                carry[g, over(b), :] = state
                state = fade * state + jnp.where(own_modes, ends[over(b)], 0.0)
            states[my_ctx, pl.ds(g, 1), :] = jnp.sum(state, axis=0, keepdims=True)

    def state_pairs(todo):
        for k, pair in enumerate(todo):
            state_pair(pair, k)

    def state_chunk(chunk, _):
        bring(3, lk_hbm, lk, chunk).wait()
        run_pairs(chunk, state_pairs)
        return 0

    lax.fori_loop(0, chunks, state_chunk, 0)

    def state_copy(slot, other):
        return pltpu.make_async_remote_copy(
            src_ref=states.at[slot],
            dst_ref=states.at[slot],
            send_sem=state_send_sem.at[other],
            recv_sem=state_recv_sem.at[slot],
            device_id={"ctx": other},
            device_id_type=pl.DeviceIdType.MESH,
        )

    def state_start(step, _):
        state_copy(my_ctx, lax.rem(my_ctx + step, n_ctx)).start()
        return 0

    lax.fori_loop(1, n_ctx, state_start, 0)

    def inner_groups(step, _):
        for g in [step * many + i for i in range(many)]:
            rows = signal[g]
            for q in range(SUB // 4):
                half = 2 * blocks
                first = rows[2 * q * half : (2 * q + 1) * half]
                second = rows[(2 * q + 1) * half : (2 * q + 2) * half]
                empty = jnp.zeros_like(first)
                mixed = jnp.dot(
                    jnp.concatenate([beside(first, empty), beside(empty, second)], axis=0),
                    bands[g, 2 * q * block : (2 * q + 2) * block, :],
                    preferred_element_type=F32,
                )
                for c in range(4):
                    side = slice((c % 2) * block, (c % 2 + 1) * block)
                    inner[g, channel_rows(4 * q + c), :] = mixed[
                        c * blocks : (c + 1) * blocks, side
                    ]
        return 0

    lax.fori_loop(0, groups // many, inner_groups, 0)

    def state_wait(step, _):
        other = lax.rem(my_ctx + step, n_ctx)
        state_copy(my_ctx, other).wait_send()
        state_copy(other, other).wait_recv()
        return 0

    lax.fori_loop(1, n_ctx, state_wait, 0)

    entering = jnp.zeros(decay_ref.shape, F32)
    device_fade = jnp.exp(-decay_ref[...] * length)
    for other in range(n_ctx - 1):
        further = device_fade * entering + states[other]
        entering = jnp.where(other < my_ctx, further, entering)
    states[0] = entering

    def out_copy(chunk):
        rows = pl.ds(pl.multiple_of(chunk * chunk_rows, 16), chunk_rows)
        return pltpu.make_async_copy(gated.at[rows], out_hbm.at[rows], out_sem.at[chunk])

    def last_pair(pair):
        rows = pl.ds(pl.multiple_of(pair * 16, 16), 16)
        query = lq[rows, :].astype(F32)
        for half in range(2):
            own = slice(half * SUB, (half + 1) * SUB)
            g = pair * 2 + half
            place = pl.ds(pl.multiple_of(pair * 16 + half * SUB, SUB), SUB)
            fade = jnp.exp(-decay_ref[pl.ds(g, 1), :] * block)
            here = jnp.where(own_modes, states[0, pl.ds(g, 1), :], 0.0)
            before = []
            for b in range(blocks):
                before.append(carry[g, over(b), :] + here)
                here = here * fade
            scale = weight_ref[pl.ds(g, 1), :] * jnp.exp(-decay_ref[pl.ds(g, 1), :])
            carried = jnp.dot(
                beside(*parts(jnp.concatenate(before, axis=0) * scale)),
                jnp.concatenate([heads[g], heads[g]], axis=0),
                preferred_element_type=F32,
            )
            carried = carried[:, :block] + carried[:, block:]
            for b in range(blocks):
                gated[place, at(b)] = query[own, at(b)] * (inner[g, over(b), :] + carried[over(b)])

    def last_pairs(todo):
        for pair in todo:
            last_pair(pair)

    def last_chunk(chunk, _):
        bring(4, lq_hbm, lq, chunk).wait()
        run_pairs(chunk, last_pairs)
        out_copy(chunk).start()
        return 0

    lax.fori_loop(0, chunks, last_chunk, 0)

    def out_wait(chunk, _):
        out_copy(chunk).wait()
        return 0

    lax.fori_loop(0, chunks, out_wait, 0)


def shards(
    short_query,
    short_key,
    short_value,
    short_taps,
    norm_gain,
    long_key,
    long_query,
    residues,
    decay_rates,
):
    channels, length = short_value.shape
    block = short_taps.shape[1]
    modes = decay_rates.shape[0]
    groups = channels // SUB
    rows = length // block * SUB
    assert modes * SUB == block
    n_ctx, n_tp = lax.axis_size("ctx"), lax.axis_size("tp")
    chunks = min(8, channels // 16)
    weights = residues * jnp.sqrt(-jnp.expm1(-2.0 * decay_rates)) * norm_gain[None, :]
    both = jnp.stack([decay_rates, weights]).transpose(0, 2, 1).reshape(2, groups, block)
    hbm = pl.BlockSpec(memory_space=pl.ANY)
    dma = pltpu.SemaphoreType.DMA
    return pl.pallas_call(
        functools.partial(fused, n_ctx, n_tp, channels * n_tp),
        out_shape=jax.ShapeDtypeStruct((channels, length), F32),
        in_specs=[hbm] * 7,
        out_specs=hbm,
        scratch_shapes=[
            pltpu.VMEM((channels, block), BF16),
            pltpu.VMEM((2, groups, block), F32),
        ]
        + [pltpu.VMEM((channels, length), BF16)] * 5
        + [pltpu.VMEM((channels, block), BF16)] * 4
        + [
            pltpu.VMEM((channels, length), F32),
            pltpu.VMEM((SUB, length), F32),
            pltpu.VMEM((n_tp, 1, length), F32),
            pltpu.VMEM((groups, rows, block), BF16),
            pltpu.VMEM((groups, block, 2 * block), BF16),
            pltpu.VMEM((groups, block, 2 * block), BF16),
            pltpu.VMEM((groups, SUB // 2 * block, 2 * block), BF16),
            pltpu.VMEM((groups, rows, block), F32),
            pltpu.VMEM((groups, rows, block), F32),
            pltpu.VMEM((8, rows + SUB, block), F32),
            pltpu.VMEM((8, rows, block), F32),
            pltpu.VMEM((n_ctx, groups, block), F32),
            dma((5, chunks)),
            dma((2,)),
            dma((2,)),
            dma((chunks,)),
            dma((2,)),
            dma((n_tp,)),
            dma((n_tp,)),
            dma((n_ctx,)),
            dma((n_ctx,)),
        ],
        compiler_params=pltpu.CompilerParams(
            collective_id=0, has_side_effects=True, vmem_limit_bytes=56 * 1024 * 1024
        ),
    )(
        short_query,
        short_key,
        short_value,
        long_key,
        long_query,
        short_taps,
        both,
    )


def solution(mesh):
    in_specs = (
        P("tp", "ctx"),
        P("tp", "ctx"),
        P("tp", "ctx"),
        P("tp", None),
        P("tp"),
        P("tp", "ctx"),
        P("tp", "ctx"),
        P(None, "tp"),
        P(None, "tp"),
    )
    out_specs = P("tp", "ctx")
    return jax.shard_map(shards, mesh=mesh, in_specs=in_specs, out_specs=out_specs, check_vma=False)
```

```python
import functools

import jax
import jax.numpy as jnp
from jax import lax
from jax.experimental import pallas as pl
from jax.experimental.pallas import tpu as pltpu
from jax.sharding import PartitionSpec as P

F32 = jnp.float32
BF16 = jnp.bfloat16
SUB = 8


def fused(
    n_ctx,
    n_tp,
    width,
    sq_hbm,
    sk_hbm,
    sv_hbm,
    lk_hbm,
    taps_hbm,
    modes_hbm,
    inner_hbm,
    carry_hbm,
    heads_hbm,
    entering_hbm,
    taps_ref,
    modes_ref,
    sq,
    sk,
    sv,
    lk,
    key_edge,
    value_edge,
    edge_send,
    edge_recv,
    gated,
    squares,
    sums,
    signal,
    tails,
    heads,
    bands,
    carry,
    inner,
    turn_in,
    turn_out,
    states,
    in_sem,
    edge_in_sem,
    small_sem,
    out_sem,
    edge_sem,
    sum_send_sem,
    sum_recv_sem,
    state_send_sem,
    state_recv_sem,
):
    channels, length = gated.shape
    block = taps_ref.shape[1]
    blocks = length // block
    groups = channels // SUB
    chunks = in_sem.shape[1]
    chunk_rows = channels // chunks
    pairs = chunk_rows // 16
    per = min(2, pairs)
    my_ctx = lax.axis_index("ctx")
    my_tp = lax.axis_index("tp")

    def edge_in(which, source, target):
        return pltpu.make_async_copy(
            source.at[:, pl.ds(length - block, block)], target, edge_in_sem.at[which]
        )

    def small_in(which, source, target):
        return pltpu.make_async_copy(source, target, small_sem.at[which])

    def bring(which, source, target, chunk):
        rows = pl.ds(pl.multiple_of(chunk * chunk_rows, 16), chunk_rows)
        return pltpu.make_async_copy(source.at[rows], target.at[rows], in_sem.at[which, chunk])

    edge_in(0, sk_hbm, key_edge).start()
    edge_in(1, sv_hbm, value_edge).start()
    small_in(0, taps_hbm, taps_ref).start()
    small_in(1, modes_hbm, modes_ref).start()
    decay_ref, weight_ref = modes_ref.at[0], modes_ref.at[1]

    def start_short(chunk, _):
        bring(0, sk_hbm, sk, chunk).start()
        bring(1, sv_hbm, sv, chunk).start()
        bring(2, sq_hbm, sq, chunk).start()
        return 0

    def start_long(chunk, _):
        bring(3, lk_hbm, lk, chunk).start()
        return 0

    lax.fori_loop(0, chunks, start_short, 0)
    lax.fori_loop(0, chunks, start_long, 0)

    barrier = pltpu.get_barrier_semaphore()

    def greet_ctx(step, _):
        other = lax.rem(my_ctx + step, n_ctx)
        pl.semaphore_signal(
            barrier, inc=1, device_id={"ctx": other}, device_id_type=pl.DeviceIdType.MESH
        )
        return 0

    def greet_tp(step, _):
        other = lax.rem(my_tp + step, n_tp)
        pl.semaphore_signal(
            barrier, inc=1, device_id={"tp": other}, device_id_type=pl.DeviceIdType.MESH
        )
        return 0

    lax.fori_loop(1, n_ctx, greet_ctx, 0)
    lax.fori_loop(1, n_tp, greet_tp, 0)
    pl.semaphore_wait(barrier, n_ctx + n_tp - 2)

    edge_in(0, sk_hbm, key_edge).wait()
    edge_in(1, sv_hbm, value_edge).wait()
    edge_send[...] = (key_edge[...].astype(F32) * value_edge[...].astype(F32)).astype(BF16)
    edge_copy = pltpu.make_async_remote_copy(
        src_ref=edge_send,
        dst_ref=edge_recv,
        send_sem=edge_sem.at[0],
        recv_sem=edge_sem.at[1],
        device_id={"ctx": lax.rem(my_ctx + 1, n_ctx)},
        device_id_type=pl.DeviceIdType.MESH,
    )
    edge_copy.start()

    row_id = lax.broadcasted_iota(jnp.int32, (block, block), 0)
    col_id = lax.broadcasted_iota(jnp.int32, (block, block), 1)
    lower_mask = jnp.where(col_id >= row_id, 1.0, 0.0).astype(BF16)
    upper_mask = jnp.where(col_id < row_id, 1.0, 0.0).astype(BF16)
    sub_id = lax.broadcasted_iota(jnp.int32, (SUB, block), 0)
    lane_id = lax.broadcasted_iota(jnp.int32, (SUB, block), 1)
    own_modes = (lane_id // (block // SUB)) == sub_id

    def beside(left, right):
        return jnp.concatenate([left, right], axis=1)

    def channel_rows(first):
        return pl.ds(first, blocks, stride=SUB)

    def circulant(row):
        base = jnp.broadcast_to(row, (16, block))
        base = pltpu.roll(base, 0, 1, stride=1, stride_axis=0).astype(BF16)
        turned = [base] + [pltpu.roll(base, 16 * a, 1) for a in range(1, block // 16)]
        return jnp.concatenate(turned, axis=0)

    def parts(value):
        high = value.astype(BF16)
        return high, (value - high.astype(F32)).astype(BF16)

    def run_pairs(chunk, body):
        def step(i, _):
            body([chunk * pairs + i * per + k for k in range(per)])
            return 0

        lax.fori_loop(0, pairs // per, step, 0)

    def at(b):
        return slice(b * block, (b + 1) * block)

    def over(b):
        return slice(b * SUB, (b + 1) * SUB)

    step_at = col_id.astype(F32)

    def make_params(step, _):
        for g in [step * 4 + i for i in range(4)]:
            decay = jnp.broadcast_to(decay_ref[pl.ds(g, 1), :], (block, block)).T
            tail = beside(*parts(jnp.exp(-decay * (block - 1 - step_at))))
            head = beside(*parts(jnp.exp(-decay * step_at)))
            weight = jnp.where(own_modes, weight_ref[pl.ds(g, 1), :], 0.0)
            sums_two = jnp.dot(
                beside(*parts(weight)),
                jnp.concatenate([head, head], axis=0),
                preferred_element_type=F32,
            )
            kernel = sums_two[:, :block] + sums_two[:, block:]
            band = [circulant(kernel[c : c + 1]) * lower_mask for c in range(SUB)]
            tails[g] = tail
            heads[g] = head
            for s in range(SUB // 2):
                bands[g, s * block : (s + 1) * block, :] = beside(band[2 * s], band[2 * s + 1])
        return 0

    small_in(0, taps_hbm, taps_ref).wait()
    small_in(1, modes_hbm, modes_ref).wait()
    lax.fori_loop(0, groups // 8, make_params, 0)

    squares[...] = jnp.zeros_like(squares)
    edge_copy.wait()
    def entering_out():
        return pltpu.make_async_copy(states.at[0], entering_hbm, out_sem.at[0])

    def heads_out():
        return pltpu.make_async_copy(heads, heads_hbm, out_sem.at[1])

    def carry_out():
        return pltpu.make_async_copy(carry, carry_hbm, out_sem.at[2])

    def inner_out(step):
        some = pl.ds(step * 4, 4)
        return pltpu.make_async_copy(inner.at[some], inner_hbm.at[some], out_sem.at[3 + step])

    has_left = jnp.where(my_ctx > 0, 1.0, 0.0).astype(F32)

    def short_pairs(todo):
        places = [pl.ds(pl.multiple_of(pair * 16, 16), 16) for pair in todo]
        for k, rows in enumerate(places):
            product = sk[rows, :].astype(F32) * sv[rows, :].astype(F32)
            edge = edge_recv[rows, :].astype(F32) * has_left
            for half in range(2):
                own = slice(half * SUB, (half + 1) * SUB)
                turn_in[2 * k + half, over(0), :] = edge[own]
                for b in range(blocks):
                    turn_in[2 * k + half, over(b + 1), :] = product[own, at(b)]
        for k, rows in enumerate(places):
            taps = taps_ref[rows, :].astype(F32)
            for half in range(2):
                slot = 2 * k + half
                for s in range(SUB // 2):
                    windows, bands_now = [], []
                    for c in (2 * s, 2 * s + 1):
                        windows.append(
                            beside(
                                turn_in[slot, channel_rows(SUB + c), :].astype(BF16),
                                turn_in[slot, channel_rows(c), :].astype(BF16),
                            )
                        )
                        turned = circulant(taps[half * SUB + c : half * SUB + c + 1])
                        bands_now.append(
                            jnp.concatenate([turned * lower_mask, turned * upper_mask], axis=0)
                        )
                    mixed = jnp.dot(
                        jnp.concatenate(windows, axis=0),
                        beside(*bands_now),
                        preferred_element_type=F32,
                    )
                    turn_out[slot, channel_rows(2 * s), :] = mixed[:blocks, :block]
                    turn_out[slot, channel_rows(2 * s + 1), :] = mixed[blocks:, block:]
        queries = [sq[rows, :].astype(F32) for rows in places]
        for b in range(blocks):
            square = squares[:, at(b)]
            for k, rows in enumerate(places):
                mix = jnp.concatenate(
                    [turn_out[2 * k, over(b), :], turn_out[2 * k + 1, over(b), :]], axis=0
                )
                gate = queries[k][:, at(b)] * mix
                gated[rows, at(b)] = gate
                square = square + gate[:SUB] * gate[:SUB] + gate[SUB:] * gate[SUB:]
            squares[:, at(b)] = square

    def short_chunk(chunk, _):
        bring(0, sk_hbm, sk, chunk).wait()
        bring(1, sv_hbm, sv, chunk).wait()
        bring(2, sq_hbm, sq, chunk).wait()
        run_pairs(chunk, short_pairs)
        return 0

    lax.fori_loop(0, chunks, short_chunk, 0)

    sums[my_tp] = jnp.sum(squares[...], axis=0, keepdims=True)

    def sum_copy(slot, other):
        return pltpu.make_async_remote_copy(
            src_ref=sums.at[slot],
            dst_ref=sums.at[slot],
            send_sem=sum_send_sem.at[other],
            recv_sem=sum_recv_sem.at[slot],
            device_id={"tp": other},
            device_id_type=pl.DeviceIdType.MESH,
        )

    def sum_start(step, _):
        sum_copy(my_tp, lax.rem(my_tp + step, n_tp)).start()
        return 0

    lax.fori_loop(1, n_tp, sum_start, 0)

    lax.fori_loop(groups // 8, groups // 4, make_params, 0)
    heads_out().start()

    def sum_wait(step, _):
        other = lax.rem(my_tp + step, n_tp)
        sum_copy(my_tp, other).wait_send()
        sum_copy(other, other).wait_recv()
        return 0

    lax.fori_loop(1, n_tp, sum_wait, 0)
    total = sums[0]
    for other in range(1, n_tp):
        total = total + sums[other]
    squares[...] = jnp.broadcast_to(lax.rsqrt(total / width + 1e-06), squares.shape)

    def state_pair(pair, k):
        rows = pl.ds(pl.multiple_of(pair * 16, 16), 16)
        key = lk[rows, :].astype(F32)
        for half in range(2):
            own = slice(half * SUB, (half + 1) * SUB)
            g = pair * 2 + half
            place = pl.ds(pl.multiple_of(pair * 16 + half * SUB, SUB), SUB)
            whole = jnp.concatenate(
                [
                    key[own, at(b)] * (gated[place, at(b)] * squares[:, at(b)])
                    for b in range(blocks)
                ],
                axis=0,
            )
            stacked = whole.astype(BF16)
            turn_out[2 * k + half] = whole
            signal[g] = jnp.concatenate(
                [turn_out[2 * k + half, channel_rows(c), :] for c in range(SUB)], axis=0
            ).astype(BF16)
            ends = lax.dot_general(
                jnp.concatenate([stacked, stacked], axis=1),
                tails[g],
                (((1,), (1,)), ((), ())),
                preferred_element_type=F32,
            )
            fade = jnp.exp(-decay_ref[pl.ds(g, 1), :] * block)
            state = jnp.zeros((SUB, block), F32)
            for b in range(blocks):
                carry[g, over(b), :] = state
                state = fade * state + jnp.where(own_modes, ends[over(b)], 0.0)
            states[my_ctx, pl.ds(g, 1), :] = jnp.sum(state, axis=0, keepdims=True)

    def state_pairs(todo):
        for k, pair in enumerate(todo):
            state_pair(pair, k)

    def state_chunk(chunk, _):
        bring(3, lk_hbm, lk, chunk).wait()
        run_pairs(chunk, state_pairs)
        return 0

    lax.fori_loop(0, chunks, state_chunk, 0)
    carry_out().start()

    def state_copy(slot, other):
        return pltpu.make_async_remote_copy(
            src_ref=states.at[slot],
            dst_ref=states.at[slot],
            send_sem=state_send_sem.at[other],
            recv_sem=state_recv_sem.at[slot],
            device_id={"ctx": other},
            device_id_type=pl.DeviceIdType.MESH,
        )

    def state_start(step, _):
        state_copy(my_ctx, lax.rem(my_ctx + step, n_ctx)).start()
        return 0

    lax.fori_loop(1, n_ctx, state_start, 0)

    def inner_groups(step, _):
        for g in [step * 4 + i for i in range(4)]:
            rows = signal[g]
            for q in range(SUB // 4):
                half = 2 * blocks
                first = rows[2 * q * half : (2 * q + 1) * half]
                second = rows[(2 * q + 1) * half : (2 * q + 2) * half]
                empty = jnp.zeros_like(first)
                mixed = jnp.dot(
                    jnp.concatenate([beside(first, empty), beside(empty, second)], axis=0),
                    bands[g, 2 * q * block : (2 * q + 2) * block, :],
                    preferred_element_type=F32,
                )
                for c in range(4):
                    side = slice((c % 2) * block, (c % 2 + 1) * block)
                    inner[g, channel_rows(4 * q + c), :] = mixed[
                        c * blocks : (c + 1) * blocks, side
                    ]
        inner_out(step).start()
        return 0

    lax.fori_loop(0, groups // 4, inner_groups, 0)

    def state_wait(step, _):
        other = lax.rem(my_ctx + step, n_ctx)
        state_copy(my_ctx, other).wait_send()
        state_copy(other, other).wait_recv()
        return 0

    lax.fori_loop(1, n_ctx, state_wait, 0)

    entering = jnp.zeros(decay_ref.shape, F32)
    device_fade = jnp.exp(-decay_ref[...] * length)
    for other in range(n_ctx - 1):
        further = device_fade * entering + states[other]
        entering = jnp.where(other < my_ctx, further, entering)
    states[0] = entering
    entering_out().start()
    entering_out().wait()
    heads_out().wait()
    carry_out().wait()

    def inner_wait(step, _):
        inner_out(step).wait()
        return 0

    lax.fori_loop(0, groups // 4, inner_wait, 0)


def finish(query_ref, inner_ref, carry_ref, heads_ref, entering_ref, modes_ref, out_ref):
    here_groups, block = entering_ref.shape
    blocks = out_ref.shape[1] // block
    sub_id = lax.broadcasted_iota(jnp.int32, (SUB, block), 0)
    lane_id = lax.broadcasted_iota(jnp.int32, (SUB, block), 1)
    own_modes = (lane_id // (block // SUB)) == sub_id

    def parts(value):
        high = value.astype(BF16)
        return high, (value - high.astype(F32)).astype(BF16)

    def pair_step(pair, _):
        rows = pl.ds(pl.multiple_of(pair * 16, 16), 16)
        query = query_ref[rows, :].astype(F32)
        mixes = []
        for half in range(2):
            g = pair * 2 + half
            decay = modes_ref[0, pl.ds(g, 1), :]
            fade = jnp.exp(-decay * block)
            here = jnp.where(own_modes, entering_ref[pl.ds(g, 1), :], 0.0)
            before = []
            for b in range(blocks):
                before.append(carry_ref[g, b * SUB : (b + 1) * SUB, :] + here)
                here = here * fade
            scale = modes_ref[1, pl.ds(g, 1), :] * jnp.exp(-decay)
            head = heads_ref[g]
            carried = jnp.dot(
                jnp.concatenate(parts(jnp.concatenate(before, axis=0) * scale), axis=1),
                jnp.concatenate([head, head], axis=0),
                preferred_element_type=F32,
            )
            mixes.append(inner_ref[g] + carried[:, :block] + carried[:, block:])
        for b in range(blocks):
            own, at = slice(b * SUB, (b + 1) * SUB), slice(b * block, (b + 1) * block)
            out_ref[rows, at] = query[:, at] * jnp.concatenate([mix[own] for mix in mixes], axis=0)
        return 0

    lax.fori_loop(0, here_groups // 2, pair_step, 0, unroll=2)


def shards(
    short_query,
    short_key,
    short_value,
    short_taps,
    norm_gain,
    long_key,
    long_query,
    residues,
    decay_rates,
):
    channels, length = short_value.shape
    block = short_taps.shape[1]
    modes = decay_rates.shape[0]
    groups = channels // SUB
    rows = length // block * SUB
    assert modes * SUB == block
    n_ctx, n_tp = lax.axis_size("ctx"), lax.axis_size("tp")
    chunks = min(8, channels // 16)
    weights = residues * jnp.sqrt(-jnp.expm1(-2.0 * decay_rates)) * norm_gain[None, :]
    both = jnp.stack([decay_rates, weights]).transpose(0, 2, 1).reshape(2, groups, block)
    hbm = pl.BlockSpec(memory_space=pl.ANY)
    dma = pltpu.SemaphoreType.DMA
    inner, carry, heads, entering = pl.pallas_call(
        functools.partial(fused, n_ctx, n_tp, channels * n_tp),
        out_shape=[
            jax.ShapeDtypeStruct((groups, rows, block), F32),
            jax.ShapeDtypeStruct((groups, rows, block), F32),
            jax.ShapeDtypeStruct((groups, block, 2 * block), BF16),
            jax.ShapeDtypeStruct((groups, block), F32),
        ],
        in_specs=[hbm] * 6,
        out_specs=[hbm] * 4,
        scratch_shapes=[
            pltpu.VMEM((channels, block), BF16),
            pltpu.VMEM((2, groups, block), F32),
        ]
        + [pltpu.VMEM((channels, length), BF16)] * 4
        + [pltpu.VMEM((channels, block), BF16)] * 4
        + [
            pltpu.VMEM((channels, length), F32),
            pltpu.VMEM((SUB, length), F32),
            pltpu.VMEM((n_tp, 1, length), F32),
            pltpu.VMEM((groups, rows, block), BF16),
            pltpu.VMEM((groups, block, 2 * block), BF16),
            pltpu.VMEM((groups, block, 2 * block), BF16),
            pltpu.VMEM((groups, SUB // 2 * block, 2 * block), BF16),
            pltpu.VMEM((groups, rows, block), F32),
            pltpu.VMEM((groups, rows, block), F32),
            pltpu.VMEM((4, rows + SUB, block), F32),
            pltpu.VMEM((4, rows, block), F32),
            pltpu.VMEM((n_ctx, groups, block), F32),
            dma((4, chunks)),
            dma((2,)),
            dma((2,)),
            dma((3 + groups // 4,)),
            dma((2,)),
            dma((n_tp,)),
            dma((n_tp,)),
            dma((n_ctx,)),
            dma((n_ctx,)),
        ],
        compiler_params=pltpu.CompilerParams(
            collective_id=0, has_side_effects=True, vmem_limit_bytes=56 * 1024 * 1024
        ),
    )(
        short_query,
        short_key,
        short_value,
        long_key,
        short_taps,
        both,
    )
    own = min(8, groups)

    def block_of(array):
        rest = array.shape[1:]
        return pl.BlockSpec((own,) + rest, lambda i: (i,) + (0,) * len(rest))

    wide = pl.BlockSpec((own * SUB, length), lambda i: (i, 0))
    return pl.pallas_call(
        finish,
        grid=(groups // own,),
        out_shape=jax.ShapeDtypeStruct((channels, length), F32),
        in_specs=[
            wide,
            block_of(inner),
            block_of(carry),
            block_of(heads),
            block_of(entering),
            pl.BlockSpec((2, own, block), lambda i: (0, i, 0)),
        ],
        out_specs=wide,
        compiler_params=pltpu.CompilerParams(vmem_limit_bytes=32 * 1024 * 1024),
    )(long_query, inner, carry, heads, entering, both)


def solution(mesh):
    in_specs = (
        P("tp", "ctx"),
        P("tp", "ctx"),
        P("tp", "ctx"),
        P("tp", None),
        P("tp"),
        P("tp", "ctx"),
        P("tp", "ctx"),
        P(None, "tp"),
        P(None, "tp"),
    )
    out_specs = P("tp", "ctx")
    return jax.shard_map(shards, mesh=mesh, in_specs=in_specs, out_specs=out_specs, check_vma=False)
```

```python
import functools

import jax
import jax.numpy as jnp
from jax import lax
from jax.experimental import pallas as pl
from jax.experimental.pallas import tpu as pltpu
from jax.sharding import PartitionSpec as P

F32 = jnp.float32
BF16 = jnp.bfloat16
SUB = 8


def fused(
    n_ctx,
    n_tp,
    width,
    sq_hbm,
    sk_hbm,
    sv_hbm,
    lk_hbm,
    taps_hbm,
    modes_hbm,
    inner_hbm,
    carry_hbm,
    heads_hbm,
    entering_hbm,
    taps_ref,
    modes_ref,
    sq,
    sk,
    sv,
    lk,
    key_edge,
    value_edge,
    edge_send,
    edge_recv,
    gated,
    squares,
    sums,
    signal,
    tails,
    heads,
    bands,
    carry,
    inner,
    turn_in,
    turn_out,
    states,
    in_sem,
    edge_in_sem,
    small_sem,
    out_sem,
    edge_sem,
    sum_send_sem,
    sum_recv_sem,
    state_send_sem,
    state_recv_sem,
):
    channels, length = gated.shape
    block = taps_ref.shape[1]
    blocks = length // block
    groups = channels // SUB
    chunks = in_sem.shape[1]
    chunk_rows = channels // chunks
    pairs = chunk_rows // 16
    per = min(2, pairs)
    my_ctx = lax.axis_index("ctx")
    my_tp = lax.axis_index("tp")

    def edge_in(which, source, target):
        return pltpu.make_async_copy(
            source.at[:, pl.ds(length - block, block)], target, edge_in_sem.at[which]
        )

    def small_in(which, source, target):
        return pltpu.make_async_copy(source, target, small_sem.at[which])

    def bring(which, source, target, chunk):
        rows = pl.ds(pl.multiple_of(chunk * chunk_rows, 16), chunk_rows)
        return pltpu.make_async_copy(source.at[rows], target.at[rows], in_sem.at[which, chunk])

    edge_in(0, sk_hbm, key_edge).start()
    edge_in(1, sv_hbm, value_edge).start()
    small_in(0, taps_hbm, taps_ref).start()
    small_in(1, modes_hbm, modes_ref).start()
    decay_ref, weight_ref = modes_ref.at[0], modes_ref.at[1]

    def start_short(chunk, _):
        bring(0, sk_hbm, sk, chunk).start()
        bring(1, sv_hbm, sv, chunk).start()
        bring(2, sq_hbm, sq, chunk).start()
        return 0

    def start_long(chunk, _):
        bring(3, lk_hbm, lk, chunk).start()
        return 0

    lax.fori_loop(0, chunks, start_short, 0)
    lax.fori_loop(0, chunks, start_long, 0)

    barrier = pltpu.get_barrier_semaphore()

    def greet_ctx(step, _):
        other = lax.rem(my_ctx + step, n_ctx)
        pl.semaphore_signal(
            barrier, inc=1, device_id={"ctx": other}, device_id_type=pl.DeviceIdType.MESH
        )
        return 0

    def greet_tp(step, _):
        other = lax.rem(my_tp + step, n_tp)
        pl.semaphore_signal(
            barrier, inc=1, device_id={"tp": other}, device_id_type=pl.DeviceIdType.MESH
        )
        return 0

    lax.fori_loop(1, n_ctx, greet_ctx, 0)
    lax.fori_loop(1, n_tp, greet_tp, 0)
    pl.semaphore_wait(barrier, n_ctx + n_tp - 2)

    edge_in(0, sk_hbm, key_edge).wait()
    edge_in(1, sv_hbm, value_edge).wait()
    edge_send[...] = (key_edge[...].astype(F32) * value_edge[...].astype(F32)).astype(BF16)
    edge_copy = pltpu.make_async_remote_copy(
        src_ref=edge_send,
        dst_ref=edge_recv,
        send_sem=edge_sem.at[0],
        recv_sem=edge_sem.at[1],
        device_id={"ctx": lax.rem(my_ctx + 1, n_ctx)},
        device_id_type=pl.DeviceIdType.MESH,
    )
    edge_copy.start()

    row_id = lax.broadcasted_iota(jnp.int32, (block, block), 0)
    col_id = lax.broadcasted_iota(jnp.int32, (block, block), 1)
    lower_mask = jnp.where(col_id >= row_id, 1.0, 0.0).astype(BF16)
    upper_mask = jnp.where(col_id < row_id, 1.0, 0.0).astype(BF16)
    sub_id = lax.broadcasted_iota(jnp.int32, (SUB, block), 0)
    lane_id = lax.broadcasted_iota(jnp.int32, (SUB, block), 1)
    own_modes = (lane_id // (block // SUB)) == sub_id

    def beside(left, right):
        return jnp.concatenate([left, right], axis=1)

    def channel_rows(first):
        return pl.ds(first, blocks, stride=SUB)

    def circulant(row):
        base = jnp.broadcast_to(row, (16, block))
        base = pltpu.roll(base, 0, 1, stride=1, stride_axis=0).astype(BF16)
        turned = [base] + [pltpu.roll(base, 16 * a, 1) for a in range(1, block // 16)]
        return jnp.concatenate(turned, axis=0)

    def parts(value):
        high = value.astype(BF16)
        return high, (value - high.astype(F32)).astype(BF16)

    def run_pairs(chunk, body):
        def step(i, _):
            body([chunk * pairs + i * per + k for k in range(per)])
            return 0

        lax.fori_loop(0, pairs // per, step, 0)

    def at(b):
        return slice(b * block, (b + 1) * block)

    def over(b):
        return slice(b * SUB, (b + 1) * SUB)

    step_at = col_id.astype(F32)

    def make_params(step, _):
        for g in [step * 4 + i for i in range(4)]:
            decay = jnp.broadcast_to(decay_ref[pl.ds(g, 1), :], (block, block)).T
            tail = beside(*parts(jnp.exp(-decay * (block - 1 - step_at))))
            head = beside(*parts(jnp.exp(-decay * step_at)))
            weight = jnp.where(own_modes, weight_ref[pl.ds(g, 1), :], 0.0)
            sums_two = jnp.dot(
                beside(*parts(weight)),
                jnp.concatenate([head, head], axis=0),
                preferred_element_type=F32,
            )
            kernel = sums_two[:, :block] + sums_two[:, block:]
            band = [circulant(kernel[c : c + 1]) * lower_mask for c in range(SUB)]
            tails[g] = tail
            heads[g] = head
            for s in range(SUB // 2):
                bands[g, s * block : (s + 1) * block, :] = beside(band[2 * s], band[2 * s + 1])
        return 0

    small_in(0, taps_hbm, taps_ref).wait()
    small_in(1, modes_hbm, modes_ref).wait()
    lax.fori_loop(0, groups // 8, make_params, 0)

    squares[...] = jnp.zeros_like(squares)
    edge_copy.wait()
    def entering_out():
        return pltpu.make_async_copy(states.at[0], entering_hbm, out_sem.at[0])

    def heads_out():
        return pltpu.make_async_copy(heads, heads_hbm, out_sem.at[1])

    def carry_out():
        return pltpu.make_async_copy(carry, carry_hbm, out_sem.at[2])

    def inner_out(step):
        some = pl.ds(step * 4, 4)
        return pltpu.make_async_copy(inner.at[some], inner_hbm.at[some], out_sem.at[3 + step])

    has_left = jnp.where(my_ctx > 0, 1.0, 0.0).astype(F32)

    def short_pairs(todo):
        places = [pl.ds(pl.multiple_of(pair * 16, 16), 16) for pair in todo]
        for k, rows in enumerate(places):
            product = sk[rows, :].astype(F32) * sv[rows, :].astype(F32)
            edge = edge_recv[rows, :].astype(F32) * has_left
            for half in range(2):
                own = slice(half * SUB, (half + 1) * SUB)
                turn_in[2 * k + half, over(0), :] = edge[own]
                for b in range(blocks):
                    turn_in[2 * k + half, over(b + 1), :] = product[own, at(b)]
        for k, rows in enumerate(places):
            taps = taps_ref[rows, :].astype(F32)
            for half in range(2):
                slot = 2 * k + half
                for s in range(SUB // 2):
                    windows, bands_now = [], []
                    for c in (2 * s, 2 * s + 1):
                        windows.append(
                            beside(
                                turn_in[slot, channel_rows(SUB + c), :].astype(BF16),
                                turn_in[slot, channel_rows(c), :].astype(BF16),
                            )
                        )
                        turned = circulant(taps[half * SUB + c : half * SUB + c + 1])
                        bands_now.append(
                            jnp.concatenate([turned * lower_mask, turned * upper_mask], axis=0)
                        )
                    mixed = jnp.dot(
                        jnp.concatenate(windows, axis=0),
                        beside(*bands_now),
                        preferred_element_type=F32,
                    )
                    turn_out[slot, channel_rows(2 * s), :] = mixed[:blocks, :block]
                    turn_out[slot, channel_rows(2 * s + 1), :] = mixed[blocks:, block:]
        queries = [sq[rows, :].astype(F32) for rows in places]
        for b in range(blocks):
            square = squares[:, at(b)]
            for k, rows in enumerate(places):
                mix = jnp.concatenate(
                    [turn_out[2 * k, over(b), :], turn_out[2 * k + 1, over(b), :]], axis=0
                )
                gate = queries[k][:, at(b)] * mix
                gated[rows, at(b)] = gate
                square = square + gate[:SUB] * gate[:SUB] + gate[SUB:] * gate[SUB:]
            squares[:, at(b)] = square

    def short_chunk(chunk, _):
        bring(0, sk_hbm, sk, chunk).wait()
        bring(1, sv_hbm, sv, chunk).wait()
        bring(2, sq_hbm, sq, chunk).wait()
        run_pairs(chunk, short_pairs)
        return 0

    lax.fori_loop(0, chunks, short_chunk, 0)

    sums[my_tp] = jnp.sum(squares[...], axis=0, keepdims=True)

    def sum_copy(slot, other):
        return pltpu.make_async_remote_copy(
            src_ref=sums.at[slot],
            dst_ref=sums.at[slot],
            send_sem=sum_send_sem.at[other],
            recv_sem=sum_recv_sem.at[slot],
            device_id={"tp": other},
            device_id_type=pl.DeviceIdType.MESH,
        )

    def sum_start(step, _):
        sum_copy(my_tp, lax.rem(my_tp + step, n_tp)).start()
        return 0

    lax.fori_loop(1, n_tp, sum_start, 0)

    lax.fori_loop(groups // 8, groups // 4, make_params, 0)
    heads_out().start()

    def sum_wait(step, _):
        other = lax.rem(my_tp + step, n_tp)
        sum_copy(my_tp, other).wait_send()
        sum_copy(other, other).wait_recv()
        return 0

    lax.fori_loop(1, n_tp, sum_wait, 0)
    total = sums[0]
    for other in range(1, n_tp):
        total = total + sums[other]
    squares[...] = jnp.broadcast_to(lax.rsqrt(total / width + 1e-06), squares.shape)

    def state_pair(pair, k):
        rows = pl.ds(pl.multiple_of(pair * 16, 16), 16)
        key = lk[rows, :].astype(F32)
        for half in range(2):
            own = slice(half * SUB, (half + 1) * SUB)
            g = pair * 2 + half
            place = pl.ds(pl.multiple_of(pair * 16 + half * SUB, SUB), SUB)
            whole = jnp.concatenate(
                [
                    key[own, at(b)] * (gated[place, at(b)] * squares[:, at(b)])
                    for b in range(blocks)
                ],
                axis=0,
            )
            stacked = whole.astype(BF16)
            turn_out[2 * k + half] = whole
            signal[g] = jnp.concatenate(
                [turn_out[2 * k + half, channel_rows(c), :] for c in range(SUB)], axis=0
            ).astype(BF16)
            ends = lax.dot_general(
                jnp.concatenate([stacked, stacked], axis=1),
                tails[g],
                (((1,), (1,)), ((), ())),
                preferred_element_type=F32,
            )
            fade = jnp.exp(-decay_ref[pl.ds(g, 1), :] * block)
            state = jnp.zeros((SUB, block), F32)
            for b in range(blocks):
                carry[g, over(b), :] = state
                state = fade * state + jnp.where(own_modes, ends[over(b)], 0.0)
            states[my_ctx, pl.ds(g, 1), :] = jnp.sum(state, axis=0, keepdims=True)

    def state_pairs(todo):
        for k, pair in enumerate(todo):
            state_pair(pair, k)

    def state_chunk(chunk, _):
        bring(3, lk_hbm, lk, chunk).wait()
        run_pairs(chunk, state_pairs)
        return 0

    lax.fori_loop(0, chunks, state_chunk, 0)
    carry_out().start()

    def state_copy(slot, other):
        return pltpu.make_async_remote_copy(
            src_ref=states.at[slot],
            dst_ref=states.at[slot],
            send_sem=state_send_sem.at[other],
            recv_sem=state_recv_sem.at[slot],
            device_id={"ctx": other},
            device_id_type=pl.DeviceIdType.MESH,
        )

    def state_start(step, _):
        state_copy(my_ctx, lax.rem(my_ctx + step, n_ctx)).start()
        return 0

    lax.fori_loop(1, n_ctx, state_start, 0)

    def inner_groups(step, _):
        for g in [step * 4 + i for i in range(4)]:
            rows = signal[g]
            for q in range(SUB // 4):
                half = 2 * blocks
                first = rows[2 * q * half : (2 * q + 1) * half]
                second = rows[(2 * q + 1) * half : (2 * q + 2) * half]
                empty = jnp.zeros_like(first)
                mixed = jnp.dot(
                    jnp.concatenate([beside(first, empty), beside(empty, second)], axis=0),
                    bands[g, 2 * q * block : (2 * q + 2) * block, :],
                    preferred_element_type=F32,
                )
                for c in range(4):
                    side = slice((c % 2) * block, (c % 2 + 1) * block)
                    inner[g, channel_rows(4 * q + c), :] = mixed[
                        c * blocks : (c + 1) * blocks, side
                    ]
        inner_out(step).start()
        return 0

    lax.fori_loop(0, groups // 4, inner_groups, 0)

    def state_wait(step, _):
        other = lax.rem(my_ctx + step, n_ctx)
        state_copy(my_ctx, other).wait_send()
        state_copy(other, other).wait_recv()
        return 0

    lax.fori_loop(1, n_ctx, state_wait, 0)

    entering = jnp.zeros(decay_ref.shape, F32)
    device_fade = jnp.exp(-decay_ref[...] * length)
    for other in range(n_ctx - 1):
        further = device_fade * entering + states[other]
        entering = jnp.where(other < my_ctx, further, entering)
    states[0] = entering
    entering_out().start()
    entering_out().wait()
    heads_out().wait()
    carry_out().wait()

    def inner_wait(step, _):
        inner_out(step).wait()
        return 0

    lax.fori_loop(0, groups // 4, inner_wait, 0)


def finish(query_ref, inner_ref, carry_ref, heads_ref, entering_ref, modes_ref, out_ref):
    here_groups, block = entering_ref.shape
    blocks = out_ref.shape[1] // block
    sub_id = lax.broadcasted_iota(jnp.int32, (SUB, block), 0)
    lane_id = lax.broadcasted_iota(jnp.int32, (SUB, block), 1)
    own_modes = (lane_id // (block // SUB)) == sub_id

    def parts(value):
        high = value.astype(BF16)
        return high, (value - high.astype(F32)).astype(BF16)

    def pair_step(pair, _):
        rows = pl.ds(pl.multiple_of(pair * 16, 16), 16)
        query = query_ref[rows, :].astype(F32)
        mixes = []
        for half in range(2):
            g = pair * 2 + half
            decay = modes_ref[0, pl.ds(g, 1), :]
            fade = jnp.exp(-decay * block)
            here = jnp.where(own_modes, entering_ref[pl.ds(g, 1), :], 0.0)
            before = []
            for b in range(blocks):
                before.append(carry_ref[g, b * SUB : (b + 1) * SUB, :] + here)
                here = here * fade
            scale = modes_ref[1, pl.ds(g, 1), :] * jnp.exp(-decay)
            head = heads_ref[g]
            carried = jnp.dot(
                jnp.concatenate(parts(jnp.concatenate(before, axis=0) * scale), axis=1),
                jnp.concatenate([head, head], axis=0),
                preferred_element_type=F32,
            )
            mixes.append(inner_ref[g] + carried[:, :block] + carried[:, block:])
        for b in range(blocks):
            own, at = slice(b * SUB, (b + 1) * SUB), slice(b * block, (b + 1) * block)
            out_ref[rows, at] = query[:, at] * jnp.concatenate([mix[own] for mix in mixes], axis=0)
        return 0

    lax.fori_loop(0, here_groups // 2, pair_step, 0, unroll=2)


def shards(
    short_query,
    short_key,
    short_value,
    short_taps,
    norm_gain,
    long_key,
    long_query,
    residues,
    decay_rates,
):
    channels, length = short_value.shape
    block = short_taps.shape[1]
    modes = decay_rates.shape[0]
    groups = channels // SUB
    rows = length // block * SUB
    assert modes * SUB == block
    n_ctx, n_tp = lax.axis_size("ctx"), lax.axis_size("tp")
    chunks = min(8, channels // 16)
    weights = residues * jnp.sqrt(-jnp.expm1(-2.0 * decay_rates)) * norm_gain[None, :]
    both = jnp.stack([decay_rates, weights]).transpose(0, 2, 1).reshape(2, groups, block)
    hbm = pl.BlockSpec(memory_space=pl.ANY)
    dma = pltpu.SemaphoreType.DMA
    inner, carry, heads, entering = pl.pallas_call(
        functools.partial(fused, n_ctx, n_tp, channels * n_tp),
        out_shape=[
            jax.ShapeDtypeStruct((groups, rows, block), F32),
            jax.ShapeDtypeStruct((groups, rows, block), F32),
            jax.ShapeDtypeStruct((groups, block, 2 * block), BF16),
            jax.ShapeDtypeStruct((groups, block), F32),
        ],
        in_specs=[hbm] * 6,
        out_specs=[hbm] * 4,
        scratch_shapes=[
            pltpu.VMEM((channels, block), BF16),
            pltpu.VMEM((2, groups, block), F32),
        ]
        + [pltpu.VMEM((channels, length), BF16)] * 4
        + [pltpu.VMEM((channels, block), BF16)] * 4
        + [
            pltpu.VMEM((channels, length), F32),
            pltpu.VMEM((SUB, length), F32),
            pltpu.VMEM((n_tp, 1, length), F32),
            pltpu.VMEM((groups, rows, block), BF16),
            pltpu.VMEM((groups, block, 2 * block), BF16),
            pltpu.VMEM((groups, block, 2 * block), BF16),
            pltpu.VMEM((groups, SUB // 2 * block, 2 * block), BF16),
            pltpu.VMEM((groups, rows, block), F32),
            pltpu.VMEM((groups, rows, block), F32),
            pltpu.VMEM((4, rows + SUB, block), F32),
            pltpu.VMEM((4, rows, block), F32),
            pltpu.VMEM((n_ctx, groups, block), F32),
            dma((4, chunks)),
            dma((2,)),
            dma((2,)),
            dma((3 + groups // 4,)),
            dma((2,)),
            dma((n_tp,)),
            dma((n_tp,)),
            dma((n_ctx,)),
            dma((n_ctx,)),
        ],
        compiler_params=pltpu.CompilerParams(
            collective_id=0, has_side_effects=True, vmem_limit_bytes=56 * 1024 * 1024
        ),
    )(
        short_query,
        short_key,
        short_value,
        long_key,
        short_taps,
        both,
    )
    own = min(8, groups)

    def block_of(array):
        rest = array.shape[1:]
        return pl.BlockSpec((own,) + rest, lambda i: (i,) + (0,) * len(rest))

    wide = pl.BlockSpec((own * SUB, length), lambda i: (i, 0))
    return pl.pallas_call(
        finish,
        grid=(groups // own,),
        out_shape=jax.ShapeDtypeStruct((channels, length), F32),
        in_specs=[
            wide,
            block_of(inner),
            block_of(carry),
            block_of(heads),
            block_of(entering),
            pl.BlockSpec((2, own, block), lambda i: (0, i, 0)),
        ],
        out_specs=wide,
        compiler_params=pltpu.CompilerParams(vmem_limit_bytes=60 * 1024 * 1024),
    )(long_query, inner, carry, heads, entering, both)


def solution(mesh):
    in_specs = (
        P("tp", "ctx"),
        P("tp", "ctx"),
        P("tp", "ctx"),
        P("tp", None),
        P("tp"),
        P("tp", "ctx"),
        P("tp", "ctx"),
        P(None, "tp"),
        P(None, "tp"),
    )
    out_specs = P("tp", "ctx")
    return jax.shard_map(shards, mesh=mesh, in_specs=in_specs, out_specs=out_specs, check_vma=False)
```
